512 devices in a mesh: space: 32 (over y_lo, x, core), member: 16 (over z, y_hi).
Axes of the slice: x: 4, y: 8 (y_hi: 2, y_lo: 4; y = y_hi * 4 + y_lo), z: 8, core: 2. Of those that a mesh axis runs over, the one named last changes fastest.
Arguments:
- anomalies: bfloat16 [256, 256, 256], P('member', 'space'), may hold values from -6 to 6
- loc_blocks: bfloat16 [5, 256, 256], replicated, may hold values from -2 to 2
- tile_reach: int32 [256], P('space'), may hold values from 1 to 4, as said below
- obs_var: float32 [256, 256], P('space', 'member'), may hold values from 0.5 to 2
- innovations: float32 [2, 256, 256], P(None, 'space', 'member'), may hold values from -40 to 40
Outputs:
- increment: float32 [2, 256, 256], P(None, 'space', 'member')
- residual: float32 [2, 256, 256], P(None, 'space', 'member')
The draws below stay inside these ranges and needn't reach their ends.
Inputs may be any that keep to these rules, and one draw needn't show every extreme that they name: `tile_reach`: some tile has reach 4 and some tile has reach 1.
All inputs are finite; a program needn't handle non-finite values.
Results may differ from the reference program's by a relative error of at most 0.02.
Values may be sent and summed in bfloat16 or wider, within the bound.
No kernel may reach another device: no remote copies, remote signals or barrier semaphores. Data moves between devices by JAX's collectives and lax.ppermute only.
A program may use at most 64 MiB of HBM per device.

```python
import math
import jax
import jax.numpy as jnp
from jax import lax

TC = 256
W = 4
ITERS = 3
TILES = 256
MEMBERS = 256


def draw_loc_blocks(key, part):
    key = jax.random.fold_in(key, 5)
    noise_key, diag_key = jax.random.split(key)
    array_shape = (W + 1, TC, TC)
    noise_draw = jnp.clip(jax.random.normal(noise_key, array_shape, jnp.float32), -6.0, 6.0)
    offsets = jnp.arange(W + 1).astype(jnp.float32)
    decay_rate = 0.6 * (1.0 - 0.5 * offsets / W) / math.sqrt(TC)
    blocks = noise_draw * decay_rate[:, None, None]
    diagonal = jax.random.uniform(diag_key, (TC,), jnp.float32, 0.7, 1.3)
    return blocks.at[0].add(jnp.diag(diagonal)).astype(jnp.bfloat16)


def draw_tile_reach(key, part):
    key = jax.random.fold_in(key, 11)
    value_key, order_key = jax.random.split(key)
    reaches = jax.random.randint(value_key, (TILES,), 1, W + 1, jnp.int32)
    ordering = jax.random.permutation(order_key, TILES)
    reaches = reaches.at[ordering[0]].set(W)
    reaches = reaches.at[ordering[1]].set(1)
    return reaches.astype(jnp.int32)


def draw_innovations(key, part):
    key = jax.random.fold_in(key, 9)
    value_key, tile_key, cell_key = jax.random.split(key, 3)
    array_shape = (2, TILES, TC)
    values = jnp.clip(jax.random.normal(value_key, array_shape, jnp.float32), -6.0, 6.0)
    tile_scale = jnp.exp(jax.random.uniform(tile_key, (1, TILES, 1), jnp.float32, math.log(0.3), math.log(3.0)))
    cell_scale = jnp.exp(jax.random.uniform(cell_key, (1, 1, TC), jnp.float32, math.log(0.5), math.log(2.0)))
    return values * tile_scale * cell_scale


def block_levels(key, extent, cuts, smallest, top_value):
    level, own = 1.0, jax.random.fold_in(key, 6)
    for position, parts in cuts:
        draws = jnp.exp(jax.random.uniform(jax.random.fold_in(own, position), (parts,), jnp.float32, smallest / len(cuts), top_value / len(cuts)))
        level = level * jnp.repeat(draws, extent[position] // parts).reshape([-1 if axis == position else 1 for axis in range(len(extent))])
    return level


def noise(stream_key, dims, width, bound, pieces=(), kind=jnp.bfloat16):
    gain = block_levels(stream_key, dims, pieces, -0.22, 0.18) if pieces else 1.0
    values = jax.random.normal(stream_key, dims, jnp.float32) * width * gain
    return jnp.minimum(jnp.maximum(values, -bound), bound).astype(kind)


def setup_inputs(seed: int = 0) -> dict:
    seeds = jax.random.split(jax.random.key(seed), 6)
    return {
        "anomalies": noise(seeds[0], (MEMBERS, TILES, TC), 1.0, 6.0, ((0, 16), (1, 32))),
        "loc_blocks": draw_loc_blocks(jax.random.fold_in(seeds[5], 71), 0),
        "tile_reach": draw_tile_reach(jax.random.fold_in(seeds[5], 71), 0),
        "obs_var": jnp.clip(jnp.exp(math.log(2.0) - 1.3862944 * jax.random.uniform(seeds[3], (TILES, TC), jnp.float32) ** block_levels(seeds[3], (TILES, TC), ((0, 32), (1, 16)), -0.2, 0.2)), 0.5, 2.0),
        "innovations": draw_innovations(jax.random.fold_in(seeds[5], 71), 0),
    }


epsilon = 1e-6


def apply_block(tiles_in, matrix, transposed):
    flattened = tiles_in.reshape(-1, tiles_in.shape[-1])
    if transposed:
        result = lax.dot_general(flattened, matrix, (((1,), (1,)), ((), ())), preferred_element_type=jnp.float32)
    else:
        result = jnp.dot(flattened, matrix, preferred_element_type=jnp.float32)
    return result.reshape(tiles_in.shape)


def covariance_image(anomalies, loc_blocks, active, obs_var, direction):
    spread = anomalies.astype(jnp.float32)
    weighted = (spread[:, None] * direction[None]).astype(jnp.bfloat16)
    forward = jnp.zeros(weighted.shape, jnp.float32)
    for offset in range(W + 1):
        gated_rows = weighted * active[:, offset].astype(jnp.bfloat16)[None, None, :, None]
        forward = forward + jnp.roll(apply_block(gated_rows, loc_blocks[offset], False), offset, axis=2)
    forward = forward.astype(jnp.bfloat16)
    backward = jnp.zeros(weighted.shape, jnp.float32)
    for offset in range(W + 1):
        moved = jnp.roll(forward, -offset, axis=2)
        gate_values = active[:, offset].astype(jnp.float32)[None, None, :, None]
        backward = backward + apply_block(moved, loc_blocks[offset], True) * gate_values
    return jnp.sum(spread[:, None] * backward, axis=0) / (MEMBERS - 1) + obs_var[None] * direction


def reference(anomalies, loc_blocks, tile_reach, obs_var, innovations):
    active = jnp.arange(W + 1, dtype=jnp.int32)[None, :] <= tile_reach[:, None]
    increment = jnp.zeros(innovations.shape, jnp.float32)
    residual = innovations
    direction = innovations
    norm_now = jnp.sum(residual * residual, axis=(1, 2))
    for iteration in range(ITERS):
        image_field = covariance_image(anomalies, loc_blocks, active, obs_var, direction)
        curvature = jnp.sum(direction * image_field, axis=(1, 2))
        step_length = norm_now / curvature
        increment = increment + step_length[:, None, None] * direction
        residual = residual - step_length[:, None, None] * image_field
        if iteration + 1 < ITERS:
            norm_next = jnp.sum(residual * residual, axis=(1, 2))
            direction = residual + (norm_next / (norm_now + epsilon))[:, None, None] * direction
            norm_now = norm_next
    return increment, residual
```

```python
import jax
import jax.numpy as jnp
from jax import lax
from jax.experimental import pallas as pl
from jax.experimental.pallas import tpu as pltpu
from jax.sharding import PartitionSpec as P

W = 4
ITERS = 3
EPSILON = 1e-6
SCALE = 2.0**-8

VM = pl.BlockSpec(memory_space=pltpu.VMEM)
SM = pl.BlockSpec(memory_space=pltpu.SMEM)

BASE = [0, 5, 9, 12, 14]
BASE_T = [0, 15, 19, 22, 24]
N_TABLE = 26


def from_behind(block, axis, distance):
    n = lax.axis_size(axis)
    return lax.ppermute(block, axis, [((i - distance) % n, i) for i in range(n)])


def row_products(a, b):
    return lax.dot_general(a, b, (((1,), (1,)), ((), ())), preferred_element_type=jnp.float32)


def table_kernel(loc_ref, t_ref):
    k = 0
    for d in range(W + 1):
        total = None
        for o in range(W + 1 - d):
            p = row_products(loc_ref[o + d], loc_ref[o])
            total = p if total is None else total + p
            t_ref[k] = total
            k += 1
    for d in range(1, W + 1):
        total = None
        for o in range(W + 1 - d):
            p = row_products(loc_ref[o], loc_ref[o + d])
            total = p if total is None else total + p
            t_ref[k] = total
            k += 1
    t_ref[k] = jnp.zeros(t_ref.shape[1:], jnp.float32)


def make_tables(loc_blocks):
    return pl.pallas_call(
        table_kernel,
        out_shape=jax.ShapeDtypeStruct((N_TABLE,) + loc_blocks.shape[1:], jnp.float32),
        in_specs=[VM],
        out_specs=VM,
        compiler_params=pltpu.CompilerParams(vmem_limit_bytes=20 << 20),
    )(loc_blocks)


def apply_kernel(reach_ref, own_ref, left_ref, right_ref, t_ref, v_ref, obs_ref, y_ref, xs):
    for w in range(4):
        xs[w] = left_ref[:, 1 + w].reshape(256, 256)
        xs[4 + w] = own_ref[:, w].reshape(256, 256)
        xs[8 + w] = own_ref[:, 5 + w].reshape(256, 256)
        xs[12 + w] = right_ref[:, w].reshape(256, 256)

    def tile(w, carry):
        rows = xs[w + W].T
        reach_w = reach_ref[w + W]
        acc = [jnp.zeros((256, 128), jnp.float32) for _ in range(2)]
        for shift in range(-W, W + 1):
            d = abs(shift)
            other = w + W + shift
            covariance = jnp.dot(rows, xs[other], preferred_element_type=jnp.float32)
            reach_o = reach_ref[other]
            if shift >= 0:
                last, base = jnp.minimum(reach_o, reach_w - d), BASE[d]
            else:
                last, base = jnp.minimum(reach_w, reach_o - d), BASE_T[d]
            entry = jnp.where(last >= 0, base + last, N_TABLE - 1)
            block = covariance * t_ref[entry]
            for f in range(2):
                p = block * v_ref[f, pl.ds(other, 1), :]
                acc[f] = acc[f] + (p[:, :128] + p[:, 128:])
        for f in range(2):
            row = jnp.sum(acc[f].T, axis=0, keepdims=True)
            y_ref[f, pl.ds(w, 1), :] = (
                row * (1.0 / 255.0) + obs_ref[pl.ds(w, 1), :] * v_ref[f, pl.ds(w + W, 1), :]
            ) * SCALE
        return carry

    lax.fori_loop(0, 8, tile, 0)


def apply_operator(reach, own, left, right, table, v, obs):
    return pl.pallas_call(
        apply_kernel,
        out_shape=jax.ShapeDtypeStruct((2, 8, 256), jnp.float32),
        in_specs=[SM] + [VM] * 6,
        out_specs=VM,
        scratch_shapes=[pltpu.VMEM((16, 256, 256), jnp.bfloat16)],
        compiler_params=pltpu.CompilerParams(vmem_limit_bytes=30 << 20),
    )(reach, own, left, right, table, v, obs)


def moments_kernel(p0_ref, p1_ref, p2_ref, p3_ref, m_ref):
    p = [p0_ref, p1_ref, p2_ref, p3_ref]
    lane = lax.broadcasted_iota(jnp.int32, (1, 128), 1)
    out = jnp.zeros((1, 128), jnp.float32)
    for k in range(2 * ITERS):
        for f in range(2):
            value = jnp.sum(p[k // 2][f] * p[(k + 1) // 2][f], keepdims=True)
            out = out + jnp.where(lane == 2 * k + f, value, 0.0)
    m_ref[...] = out


def local_moments(p):
    return pl.pallas_call(
        moments_kernel,
        out_shape=jax.ShapeDtypeStruct((1, 128), jnp.float32),
        in_specs=[VM] * 4,
        out_specs=VM,
    )(*p)


def poly_add(a, b):
    n = max(len(a), len(b))
    out = []
    for i in range(n):
        if i >= len(a):
            out.append(b[i])
        elif i >= len(b):
            out.append(a[i])
        else:
            out.append(a[i] + b[i])
    return out


def poly_dot(a, b, moment):
    total = None
    for i, x in enumerate(a):
        for j, y in enumerate(b):
            if x is None or y is None:
                continue
            term = x * y * moment[i + j]
            total = term if total is None else total + term
    return total


def finish_kernel(m_ref, p0_ref, p1_ref, p2_ref, p3_ref, inc_ref, res_ref):
    p = [p0_ref, p1_ref, p2_ref, p3_ref]
    lane = lax.broadcasted_iota(jnp.int32, (1, 128), 1)
    sums = jnp.sum(m_ref[...], axis=0, keepdims=True)
    one = jnp.ones((1, 1), jnp.float32)
    zero = jnp.zeros((1, 1), jnp.float32)
    for f in range(2):
        moment = [
            jnp.sum(jnp.where(lane == 2 * k + f, sums, 0.0), axis=1, keepdims=True)
            for k in range(2 * ITERS)
        ]
        residual, direction, increment = [one], [one], []
        norm_now = moment[0]
        for iteration in range(ITERS):
            image = [None] + direction
            step = norm_now / poly_dot(direction, image, moment)
            increment = poly_add(increment, [step * c for c in direction])
            residual = poly_add(residual, [zero] + [-step * c for c in direction])
            if iteration + 1 < ITERS:
                norm_next = poly_dot(residual, residual, moment)
                ratio = norm_next / (norm_now + EPSILON)
                direction = poly_add(residual, [ratio * c for c in direction])
                norm_now = norm_next
        inc_ref[f] = sum(c * p[i][f] for i, c in enumerate(increment)) * SCALE
        res_ref[f] = sum(c * p[i][f] for i, c in enumerate(residual))


def finish(m, p):
    shape = jax.ShapeDtypeStruct(p[0].shape, jnp.float32)
    return pl.pallas_call(
        finish_kernel,
        out_shape=(shape, shape),
        in_specs=[VM] * 5,
        out_specs=(VM, VM),
    )(m, *p)


def three_pieces(x):
    high = lax.reduce_precision(x, 8, 7)
    rest = x - high
    middle = lax.reduce_precision(rest, 8, 7)
    return jnp.stack([high, middle, rest - middle]).astype(jnp.bfloat16)


def on_device(anomalies, loc_blocks, tile_reach, obs_var, innovations):
    table = make_tables(loc_blocks)
    mine = jnp.concatenate([innovations, obs_var[None]])
    extra = jnp.concatenate([three_pieces(mine).reshape(-1), tile_reach.astype(jnp.bfloat16)])
    extra = jnp.pad(extra, (0, 4096 - extra.shape[0])).reshape(1, 16, 256)
    by_tile = anomalies.transpose(1, 0, 2)
    chunk = jnp.concatenate([by_tile[:4], extra, by_tile[4:]])
    own = lax.all_to_all(jnp.broadcast_to(chunk[None], (16,) + chunk.shape), "member", 0, 0)
    left = from_behind(own[:, 4:], "space", 1)
    right = from_behind(own[:, :5], "space", -1)
    extras = jnp.stack([left[:, 0], own[:, 4], right[:, 4]]).reshape(3, 16, 4096)
    reaches = extras[:, 0, 1152:1160].astype(jnp.int32)
    reach = jnp.concatenate([reaches[0, 4:], reaches[1], reaches[2, :4]])
    pieces = extras[:, :, :1152].astype(jnp.float32).reshape(3, 16, 3, 3, 8, 16)
    values = pieces[:, :, 0] + (pieces[:, :, 1] + pieces[:, :, 2])
    values = values.transpose(0, 2, 3, 1, 4).reshape(3, 3, 8, 256)
    obs = values[1, 2]
    v = jnp.concatenate([values[0, :2, 4:], values[1, :2], values[2, :2, :4]], axis=1)
    p = [values[1, :2]]
    for power in range(ITERS):
        if power:
            before = from_behind(p[-1][:, 4:], "space", 1)
            after = from_behind(p[-1][:, :4], "space", -1)
            v = jnp.concatenate([before, p[-1], after], axis=1)
        p.append(apply_operator(reach, own, left, right, table, v, obs))
    m = local_moments(p)
    m = lax.all_to_all(jnp.broadcast_to(m, (32, 128)), "space", 0, 0, tiled=True)
    increment, residual = finish(m, p)
    start = lax.axis_index("member") * 16
    return (
        lax.dynamic_slice_in_dim(increment, start, 16, 2),
        lax.dynamic_slice_in_dim(residual, start, 16, 2),
    )


def solution(mesh):
    in_specs = (
        P("member", "space", None),
        P(),
        P("space"),
        P("space", "member"),
        P(None, "space", "member"),
    )
    out_specs = (P(None, "space", "member"), P(None, "space", "member"))
    return jax.shard_map(
        on_device, mesh=mesh, in_specs=in_specs, out_specs=out_specs, check_vma=False
    )
```

```python
import jax
import jax.numpy as jnp
from jax import lax
from jax.experimental import pallas as pl
from jax.experimental.pallas import tpu as pltpu
from jax.sharding import PartitionSpec as P

W = 4
ITERS = 3
EPSILON = 1e-6
SCALE = 2.0**-8
MIB = 1 << 20

VM = pl.BlockSpec(memory_space=pltpu.VMEM)
SM = pl.BlockSpec(memory_space=pltpu.SMEM)

FIELDS = 128
PART = 144
CHUNK = 272

BASE = [0, 5, 9, 12, 14]
BASE_T = [0, 15, 19, 22, 24]
N_TABLE = 26

INNER = [(w, s) for w in range(8) for s in range(-W, W + 1) if 0 <= w + s < 8]
OUTER = [(w, s) for w in range(8) for s in range(-W, W + 1) if not 0 <= w + s < 8]


def params(mib):
    return pltpu.CompilerParams(vmem_limit_bytes=mib * MIB)


def pair_swap(block, offset):
    n, m = lax.axis_size("space"), lax.axis_size("member")
    route = []
    for i in range(n):
        j = i + 1 if (i + offset) % 2 == 0 else i - 1
        for k in range(m):
            route.append((i * m + k, (j % n) * m + (k if 0 <= j < n else k ^ 1)))
    return lax.ppermute(block, ("space", "member"), route)


def pack_kernel(anomalies_ref, reach_ref, obs_ref, innovations_ref, chunk_ref):
    x = anomalies_ref[...].astype(jnp.float32)
    rows = []
    for t in range(8):
        tile = x[:, t, :]
        rows += [tile[:, :128], tile[:, 128:]]
    lane = lax.broadcasted_iota(jnp.int32, (1, 128), 1)
    lines = []
    for a in range(3):
        block = innovations_ref[a] if a < 2 else obs_ref[...]
        wide = jnp.concatenate([block, jnp.zeros((8, 112), jnp.float32)], axis=1)
        line = wide[0:1]
        for t in range(1, 8):
            line = line + pltpu.roll(wide[t : t + 1], 16 * t, 1)
        lines.append(line)
    values = jnp.concatenate(lines, axis=0)
    high = values.astype(jnp.bfloat16).astype(jnp.float32)
    rest = values - high
    middle = rest.astype(jnp.bfloat16).astype(jnp.float32)
    reach = jnp.zeros((1, 128), jnp.float32)
    for t in range(8):
        reach = reach + jnp.where(lane == t, reach_ref[t].astype(jnp.float32), 0.0)
    fields = jnp.concatenate(
        [high, middle, rest - middle, reach, jnp.zeros((6, 128), jnp.float32)], axis=0
    )
    chunk = jnp.concatenate(rows[:8] + [fields] + rows[8:], axis=0).astype(jnp.bfloat16)
    for k in range(16):
        chunk_ref[k] = chunk


def pack(anomalies, tile_reach, obs_var, innovations):
    return pl.pallas_call(
        pack_kernel,
        out_shape=jax.ShapeDtypeStruct((16, CHUNK, 128), jnp.bfloat16),
        in_specs=[VM, SM, VM, VM],
        out_specs=VM,
        compiler_params=params(8),
    )(anomalies, tile_reach, obs_var, innovations)


def swap_blocks(x):
    row = lax.broadcasted_iota(jnp.int32, (8, 128), 0)
    block = lax.broadcasted_iota(jnp.int32, (8, 128), 1) // 16
    for bit in (1, 2, 4):
        r, b = (row & bit) != 0, (block & bit) != 0
        up = pltpu.roll(pltpu.roll(x, 8 - bit, 0), 16 * bit, 1)
        down = pltpu.roll(pltpu.roll(x, bit, 0), 128 - 16 * bit, 1)
        x = jnp.where(r == b, x, jnp.where(b, up, down))
    return x


def unpack_fields(lines):
    lines = lines.astype(jnp.float32)
    out = []
    for a in range(3):
        value = lines[:, a] + (lines[:, 3 + a] + lines[:, 6 + a])
        out.append(jnp.concatenate([swap_blocks(value[:8]), swap_blocks(value[8:])], axis=1))
    return out


def row_products(a, b):
    return lax.dot_general(a, b, (((1,), (1,)), ((), ())), preferred_element_type=jnp.float32)


def tile_of(ref, row):
    return jnp.concatenate(
        [
            ref[:, pl.ds(row, 16), :].reshape(256, 128),
            ref[:, pl.ds(row + 16, 16), :].reshape(256, 128),
        ],
        axis=1,
    )


def table_entry(shift, reach_w, reach_o):
    d = abs(shift)
    if shift >= 0:
        last, base = jnp.minimum(reach_o, reach_w - d), BASE[d]
    else:
        last, base = jnp.minimum(reach_w, reach_o - d), BASE_T[d]
    return jnp.where(last >= 0, base + last, N_TABLE - 1)


def inner_kernel(reach_ref, loc_ref, own_ref, t_ref, h_ref, xs):
    for w in range(8):
        xs[w] = tile_of(own_ref, 32 * w + (16 if w >= 4 else 0))
    factor = SCALE / 255.0
    k = 0
    for d in range(W + 1):
        total = None
        for o in range(W + 1 - d):
            p = row_products(loc_ref[o + d], loc_ref[o])
            total = p if total is None else total + p
            t_ref[k] = total * factor
            k += 1
    for d in range(1, W + 1):
        total = None
        for o in range(W + 1 - d):
            p = row_products(loc_ref[o], loc_ref[o + d])
            total = p if total is None else total + p
            t_ref[k] = total * factor
            k += 1
    t_ref[k] = jnp.zeros(t_ref.shape[1:], jnp.float32)

    def tile(w, start):
        rows = xs[w].T
        for shift in range(-W, W + 1):
            other = w + shift

            @pl.when((other >= 0) & (other < 8))
            def _():
                entry = table_entry(shift, reach_ref[w], reach_ref[other])
                covariance = jnp.dot(rows, xs[other], preferred_element_type=jnp.float32)
                h_ref[w * 8 + other] = covariance * t_ref[entry]

        return start

    lax.fori_loop(0, 8, tile, 0)


def inner_blocks(reach, loc_blocks, own):
    return pl.pallas_call(
        inner_kernel,
        out_shape=(
            jax.ShapeDtypeStruct((N_TABLE, 256, 256), jnp.float32),
            jax.ShapeDtypeStruct((64, 256, 256), jnp.float32),
        ),
        in_specs=[SM, VM, VM],
        out_specs=(VM, VM),
        scratch_shapes=[pltpu.VMEM((8, 256, 256), jnp.bfloat16)],
        compiler_params=params(30),
        cost_estimate=pl.CostEstimate(
            flops=77 * 2 * 256**3, bytes_accessed=28 * MIB, transcendentals=0
        ),
    )(reach, loc_blocks, own)


def add_products(acc, block, v_rows):
    for f in range(2):
        p = block * v_rows[f]
        p = p[:, :128] + p[:, 128:]
        acc[f] = p if acc[f] is None else acc[f] + p


def row_sums(parts):
    return jnp.sum(jnp.concatenate(parts, axis=0).T, axis=0, keepdims=True)


ROWS = 64


def apply_blocks(inner_ref, outer_ref, v_ref, obs_ref, y):
    for w in range(8):
        done = [[], []]
        for c in range(0, 256, ROWS):
            acc = [None, None]
            for shift in range(-W, W + 1):
                other = w + shift
                if 0 <= other < 8:
                    block = inner_ref[w * 8 + other, c : c + ROWS, :]
                else:
                    block = outer_ref[OUTER.index((w, shift)), c : c + ROWS, :]
                rows = [v_ref[f, other + W : other + W + 1, :] for f in range(2)]
                add_products(acc, block, rows)
            for f in range(2):
                done[f].append(acc[f])
        for f in range(2):
            y[f, w : w + 1, :] = row_sums(done[f]) + (obs_ref[w : w + 1, :] * SCALE) * v_ref[
                f, w + W : w + W + 1, :
            ]


def set_sends(even, p, a_ref, b_ref):
    for f in range(2):
        low, high = p[f, :W], p[f, W:]
        a_ref[f] = jnp.where(even, high, low)
        b_ref[f] = jnp.where(even, low, high)


def first_kernel(
    reach_ref, own_ref, a_ref, b_ref, t_ref, inner_ref,
    outer_ref, p0_ref, obs_ref, p1_ref, send_a_ref, send_b_ref,
    xs, v, lines,
):
    even = lax.axis_index("space") % 2 == 0
    a_low, b_low = jnp.where(even, 0, 16), jnp.where(even, 16, 0)
    for w in range(8):
        xs[w + W] = tile_of(own_ref, 32 * w + (16 if w >= 4 else 0))
    for w in range(W):
        xs[jnp.where(even, 12, 0) + w] = tile_of(a_ref, pl.multiple_of(a_low + 32 * w, 16))
        xs[jnp.where(even, 0, 12) + w] = tile_of(b_ref, pl.multiple_of(b_low + 32 * w, 16))
    a_at = pl.multiple_of(jnp.where(even, 128, 0), 16)
    b_at = pl.multiple_of(jnp.where(even, 0, 128), 16)
    lines[0] = a_ref[:, pl.ds(a_at, 16), :]
    lines[1] = b_ref[:, pl.ds(b_at, 16), :]
    a_fields, b_fields = unpack_fields(lines[0]), unpack_fields(lines[1])
    own_fields = unpack_fields(own_ref[:, FIELDS : FIELDS + 16, :])
    for f in range(2):
        v[f, :W] = jnp.where(even, b_fields[f], a_fields[f])[W:]
        v[f, W : W + 8] = own_fields[f]
        v[f, W + 8 :] = jnp.where(even, a_fields[f], b_fields[f])[:W]
        p0_ref[f] = own_fields[f]
    obs_ref[...] = own_fields[2]

    lane = lax.broadcasted_iota(jnp.int32, (1, 128), 1)
    reach_a = lines[0, 0, 9:10, :].astype(jnp.float32)
    reach_b = lines[1, 0, 9:10, :].astype(jnp.float32)
    reach_left = jnp.where(even, reach_b, reach_a)
    reach_right = jnp.where(even, reach_a, reach_b)

    def reach_of(tile):
        if 0 <= tile < 8:
            return reach_ref[tile]
        line, at = (reach_left, tile + 8) if tile < 0 else (reach_right, tile - 8)
        return jnp.sum(jnp.where(lane == at, line, 0.0)).astype(jnp.int32)

    reach = {tile: reach_of(tile) for tile in range(-W, 8 + W)}
    for w in range(8):
        rows = xs[w + W].T
        for shift in range(-W, W + 1):
            if (w, shift) not in OUTER:
                continue
            entry = table_entry(shift, reach[w], reach[w + shift])
            covariance = jnp.dot(rows, xs[w + shift + W], preferred_element_type=jnp.float32)
            outer_ref[OUTER.index((w, shift))] = covariance * t_ref[entry]
    apply_blocks(inner_ref, outer_ref, v, obs_ref, p1_ref)
    set_sends(even, p1_ref, send_a_ref, send_b_ref)


FIELD = jax.ShapeDtypeStruct((2, 8, 256), jnp.float32)
HALO = jax.ShapeDtypeStruct((2, W, 256), jnp.float32)


def first_application(reach, own, a, b, table, inner):
    return pl.pallas_call(
        first_kernel,
        out_shape=(
            jax.ShapeDtypeStruct((len(OUTER), 256, 256), jnp.float32),
            FIELD,
            jax.ShapeDtypeStruct((8, 256), jnp.float32),
            FIELD,
            HALO,
            HALO,
        ),
        in_specs=[SM] + [VM] * 5,
        out_specs=(VM,) * 6,
        scratch_shapes=[
            pltpu.VMEM((16, 256, 256), jnp.bfloat16),
            pltpu.VMEM((2, 16, 256), jnp.float32),
            pltpu.VMEM((2, 16, 16, 128), jnp.bfloat16),
        ],
        compiler_params=params(36),
    )(reach, own, a, b, table, inner)


def fill_window(even, p_ref, a_ref, b_ref, v):
    for f in range(2):
        v[f, :W] = jnp.where(even, b_ref[f], a_ref[f])
        v[f, W : W + 8] = p_ref[f]
        v[f, W + 8 :] = jnp.where(even, a_ref[f], b_ref[f])


def next_kernel(
    p_ref, a_ref, b_ref, obs_ref, inner_ref, outer_ref, y_ref, send_a_ref, send_b_ref, v
):
    even = lax.axis_index("space") % 2 == 0
    fill_window(even, p_ref, a_ref, b_ref, v)
    apply_blocks(inner_ref, outer_ref, v, obs_ref, y_ref)
    set_sends(even, y_ref, send_a_ref, send_b_ref)


def next_application(p, a, b, obs, inner, outer):
    return pl.pallas_call(
        next_kernel,
        out_shape=(FIELD, HALO, HALO),
        in_specs=[VM] * 6,
        out_specs=(VM,) * 3,
        scratch_shapes=[pltpu.VMEM((2, 16, 256), jnp.float32)],
        compiler_params=params(30),
    )(p, a, b, obs, inner, outer)


def two_sum(a, b):
    s = a + b
    t = s - a
    return s, (a - (s - t)) + (b - t)


def halves(a):
    c = a * 4097.0
    high = c - (c - a)
    return high, a - high


def two_product(a, b):
    p = a * b
    ah, al = halves(a)
    bh, bl = halves(b)
    return p, ((ah * bh - p) + ah * bl + al * bh) + al * bl


def pair_add(x, y):
    s, e = two_sum(x[0], y[0])
    e = e + (x[1] + y[1])
    high = s + e
    return high, e - (high - s)


def pair_times(x, y):
    p, e = two_product(x[0], y[0])
    return p, e + (x[0] * y[1] + x[1] * y[0])


def last_kernel(
    p_ref, a_ref, b_ref, obs_ref, inner_ref, outer_ref, p0_ref, p1_ref, y_ref, m_ref, v
):
    even = lax.axis_index("space") % 2 == 0
    fill_window(even, p_ref, a_ref, b_ref, v)
    apply_blocks(inner_ref, outer_ref, v, obs_ref, y_ref)
    powers = [p0_ref, p1_ref, p_ref, y_ref]
    row = lax.broadcasted_iota(jnp.int32, (8, 128), 0)
    lane = lax.broadcasted_iota(jnp.int32, (8, 128), 1)
    sums = []
    for f in range(2):
        packed = [jnp.zeros((8, 128), jnp.float32)] * 2
        for k in range(2 * ITERS):
            p, e = two_product(powers[k // 2][f], powers[(k + 1) // 2][f])
            total = pair_add((p[:, :128], e[:, :128]), (p[:, 128:], e[:, 128:]))
            for shift in (4, 2, 1):
                total = pair_add(total, [pltpu.roll(x, shift, 0) for x in total])
            packed = [jnp.where(row == k, x, y) for x, y in zip(total, packed)]
        for shift in (64, 32, 16, 8, 4, 2, 1):
            packed = pair_add(packed, [pltpu.roll(x, shift, 1) for x in packed])
        sums.append(packed)
    high = jnp.where(lane < 32, sums[0][0], sums[1][0])
    low = jnp.where(lane < 96, sums[0][1], sums[1][1])
    out = jnp.where(lane < 64, high, low)
    for k in range(32):
        m_ref[k] = out


def last_application(p, a, b, obs, inner, outer, p0, p1):
    return pl.pallas_call(
        last_kernel,
        out_shape=(FIELD, jax.ShapeDtypeStruct((32, 8, 128), jnp.float32)),
        in_specs=[VM] * 8,
        out_specs=(VM,) * 2,
        scratch_shapes=[pltpu.VMEM((2, 16, 256), jnp.float32)],
        compiler_params=params(30),
    )(p, a, b, obs, inner, outer, p0, p1)


def square_dot(poly, moment):
    total = None
    for k in range(2 * len(poly) - 1):
        coefficient = None
        for i in range(len(poly)):
            j = k - i
            if i > j or j >= len(poly):
                continue
            term = two_product(poly[i], poly[j])
            if i != j:
                term = (2.0 * term[0], 2.0 * term[1])
            coefficient = term if coefficient is None else pair_add(coefficient, term)
        term = pair_times(coefficient, moment[k])
        total = term if total is None else pair_add(total, term)
    return total[0] + total[1]


def finish_kernel(m_ref, p0_ref, p1_ref, p2_ref, p3_ref, inc_ref, res_ref):
    member = lax.axis_index("member")
    s = m_ref[0]
    e = jnp.zeros((8, 128), jnp.float32)
    for k in range(1, 32):
        s, t = two_sum(s, m_ref[k])
        e = e + t
    low = e + pltpu.roll(s, 64, 1)
    moment = [(s[k : k + 1], low[k : k + 1]) for k in range(2 * ITERS)]
    one = jnp.ones((1, 128), jnp.float32)
    residual, direction, increment = [one], [one], []
    norm_now = moment[0][0] + moment[0][1]
    for iteration in range(ITERS):
        step = norm_now / square_dot(direction, moment[1:])
        moved = [step * c for c in direction]
        increment = [x + y for x, y in zip(increment, moved)] + moved[len(increment) :]
        residual = residual[:1] + [
            (residual[i + 1] if i + 1 < len(residual) else 0.0) - c for i, c in enumerate(moved)
        ]
        if iteration + 1 < ITERS:
            norm_next = square_dot(residual, moment)
            ratio = norm_next / (norm_now + EPSILON)
            grown = [ratio * c for c in direction]
            direction = [x + y for x, y in zip(residual, grown)] + residual[len(grown) :]
            norm_now = norm_next
    shift = (128 - (member % 8) * 16) % 128
    upper = member >= 8
    powers = [p0_ref, p1_ref, p2_ref, p3_ref]
    for f in range(2):
        at = 32 * f
        mine = [
            pltpu.roll(jnp.where(upper, p[f, :, 128:], p[f, :, :128]), shift, 1) for p in powers
        ]
        inc = sum(c[:, at : at + 1] * x for c, x in zip(increment, mine)) * SCALE
        res = sum(c[:, at : at + 1] * x for c, x in zip(residual, mine))
        inc_ref[f] = inc[:, :16]
        res_ref[f] = res[:, :16]


def finish(m, p):
    shape = jax.ShapeDtypeStruct((2, 8, 16), jnp.float32)
    return pl.pallas_call(
        finish_kernel,
        out_shape=(shape, shape),
        in_specs=[VM] * 5,
        out_specs=(VM, VM),
        compiler_params=params(8),
    )(m, *p)


def on_device(anomalies, loc_blocks, tile_reach, obs_var, innovations):
    chunk = pack(anomalies, tile_reach, obs_var, innovations)
    own = lax.all_to_all(chunk, "member", 0, 0)
    odd = lax.axis_index("space") % 2
    to_a = lax.dynamic_slice_in_dim(own, 128 * (1 - odd), PART, 1)
    to_b = lax.dynamic_slice_in_dim(own, 128 * odd, PART, 1)
    a, b = pair_swap(to_a, 0), pair_swap(to_b, 1)
    table, inner = inner_blocks(tile_reach, loc_blocks, own)
    outer, p0, obs, p1, to_a, to_b = first_application(tile_reach, own, a, b, table, inner)
    a, b = pair_swap(to_a, 0), pair_swap(to_b, 1)
    p2, to_a, to_b = next_application(p1, a, b, obs, inner, outer)
    a, b = pair_swap(to_a, 0), pair_swap(to_b, 1)
    p3, m = last_application(p2, a, b, obs, inner, outer, p0, p1)
    m = lax.all_to_all(m, "space", 0, 0)
    return finish(m, [p0, p1, p2, p3])


def solution(mesh):
    in_specs = (
        P("member", "space", None),
        P(),
        P("space"),
        P("space", "member"),
        P(None, "space", "member"),
    )
    out_specs = (P(None, "space", "member"), P(None, "space", "member"))
    return jax.shard_map(
        on_device, mesh=mesh, in_specs=in_specs, out_specs=out_specs, check_vma=False
    )
```

```python
import jax
import jax.numpy as jnp
from jax import lax
from jax.experimental import pallas as pl
from jax.experimental.pallas import tpu as pltpu
from jax.sharding import PartitionSpec as P

W = 4
ITERS = 3
EPSILON = 1e-6
SCALE = 2.0**-8
MIB = 1 << 20

VM = pl.BlockSpec(memory_space=pltpu.VMEM)
SM = pl.BlockSpec(memory_space=pltpu.SMEM)

FIELDS = 128
PART = 144
CHUNK = 272

BASE = [0, 5, 9, 12, 14]
BASE_T = [0, 15, 19, 22, 24]
N_TABLE = 26

INNER = [(w, s) for w in range(8) for s in range(-W, W + 1) if 0 <= w + s < 8]
OUTER = [(w, s) for w in range(8) for s in range(-W, W + 1) if not 0 <= w + s < 8]


def params(mib):
    return pltpu.CompilerParams(vmem_limit_bytes=mib * MIB)


def pair_swap(block, offset):
    n, m = lax.axis_size("space"), lax.axis_size("member")
    route = []
    for i in range(n):
        j = i + 1 if (i + offset) % 2 == 0 else i - 1
        for k in range(m):
            route.append((i * m + k, (j % n) * m + (k if 0 <= j < n else k ^ 1)))
    return lax.ppermute(block, ("space", "member"), route)


def pack_kernel(anomalies_ref, reach_ref, obs_ref, innovations_ref, chunk_ref):
    x = anomalies_ref[...].astype(jnp.float32)
    rows = []
    for t in range(8):
        tile = x[:, t, :]
        rows += [tile[:, :128], tile[:, 128:]]
    lane = lax.broadcasted_iota(jnp.int32, (1, 128), 1)
    lines = []
    for a in range(3):
        block = innovations_ref[a] if a < 2 else obs_ref[...]
        wide = jnp.concatenate([block, jnp.zeros((8, 112), jnp.float32)], axis=1)
        line = wide[0:1]
        for t in range(1, 8):
            line = line + pltpu.roll(wide[t : t + 1], 16 * t, 1)
        lines.append(line)
    values = jnp.concatenate(lines, axis=0)
    high = values.astype(jnp.bfloat16).astype(jnp.float32)
    rest = values - high
    middle = rest.astype(jnp.bfloat16).astype(jnp.float32)
    reach = jnp.zeros((1, 128), jnp.float32)
    for t in range(8):
        reach = reach + jnp.where(lane == t, reach_ref[t].astype(jnp.float32), 0.0)
    fields = jnp.concatenate(
        [high, middle, rest - middle, reach, jnp.zeros((6, 128), jnp.float32)], axis=0
    )
    chunk = jnp.concatenate(rows[:8] + [fields] + rows[8:], axis=0).astype(jnp.bfloat16)
    for k in range(16):
        chunk_ref[k] = chunk


def pack(anomalies, tile_reach, obs_var, innovations):
    return pl.pallas_call(
        pack_kernel,
        out_shape=jax.ShapeDtypeStruct((16, CHUNK, 128), jnp.bfloat16),
        in_specs=[VM, SM, VM, VM],
        out_specs=VM,
        compiler_params=params(8),
    )(anomalies, tile_reach, obs_var, innovations)


def swap_blocks(x):
    row = lax.broadcasted_iota(jnp.int32, (8, 128), 0)
    block = lax.broadcasted_iota(jnp.int32, (8, 128), 1) // 16
    for bit in (1, 2, 4):
        r, b = (row & bit) != 0, (block & bit) != 0
        up = pltpu.roll(pltpu.roll(x, 8 - bit, 0), 16 * bit, 1)
        down = pltpu.roll(pltpu.roll(x, bit, 0), 128 - 16 * bit, 1)
        x = jnp.where(r == b, x, jnp.where(b, up, down))
    return x


def unpack_fields(lines):
    lines = lines.astype(jnp.float32)
    out = []
    for a in range(3):
        value = lines[:, a] + (lines[:, 3 + a] + lines[:, 6 + a])
        out.append(jnp.concatenate([swap_blocks(value[:8]), swap_blocks(value[8:])], axis=1))
    return out


def row_products(a, b):
    return lax.dot_general(a, b, (((1,), (1,)), ((), ())), preferred_element_type=jnp.float32)


def tile_of(ref, row):
    return jnp.concatenate(
        [
            ref[:, pl.ds(row, 16), :].reshape(256, 128),
            ref[:, pl.ds(row + 16, 16), :].reshape(256, 128),
        ],
        axis=1,
    )


def table_entry(shift, reach_w, reach_o):
    d = abs(shift)
    if shift >= 0:
        last, base = jnp.minimum(reach_o, reach_w - d), BASE[d]
    else:
        last, base = jnp.minimum(reach_w, reach_o - d), BASE_T[d]
    return jnp.where(last >= 0, base + last, N_TABLE - 1)


def table_kernel(loc_ref, t_ref):
    factor = SCALE / 255.0
    k = 0
    for d in range(W + 1):
        total = None
        for o in range(W + 1 - d):
            p = row_products(loc_ref[o + d], loc_ref[o])
            total = p if total is None else total + p
            t_ref[k] = total * factor
            k += 1
    for d in range(1, W + 1):
        total = None
        for o in range(W + 1 - d):
            p = row_products(loc_ref[o], loc_ref[o + d])
            total = p if total is None else total + p
            t_ref[k] = total * factor
            k += 1
    t_ref[k] = jnp.zeros(t_ref.shape[1:], jnp.float32)


def make_tables(loc_blocks):
    return pl.pallas_call(
        table_kernel,
        out_shape=jax.ShapeDtypeStruct((N_TABLE, 256, 256), jnp.float32),
        in_specs=[VM],
        out_specs=VM,
        compiler_params=params(14),
        cost_estimate=pl.CostEstimate(
            flops=25 * 2 * 256**3, bytes_accessed=7 * MIB, transcendentals=0
        ),
    )(loc_blocks)


def inner_kernel(reach_ref, own_ref, t_ref, h_ref, xs):
    for w in range(8):
        xs[w] = tile_of(own_ref, 32 * w + (16 if w >= 4 else 0))
    for w in range(8):
        rows = xs[w].T
        for shift in range(-W, W + 1):
            if (w, shift) not in INNER:
                continue
            entry = table_entry(shift, reach_ref[w], reach_ref[w + shift])
            covariance = jnp.dot(rows, xs[w + shift], preferred_element_type=jnp.float32)
            h_ref[INNER.index((w, shift))] = covariance * t_ref[entry]


def inner_blocks(reach, own, table):
    return pl.pallas_call(
        inner_kernel,
        out_shape=jax.ShapeDtypeStruct((len(INNER), 256, 256), jnp.float32),
        in_specs=[SM, VM, VM],
        out_specs=VM,
        scratch_shapes=[pltpu.VMEM((8, 256, 256), jnp.bfloat16)],
        compiler_params=params(26),
        cost_estimate=pl.CostEstimate(
            flops=52 * 2 * 256**3, bytes_accessed=20 * MIB, transcendentals=0
        ),
    )(reach, own, table)


def add_products(acc, block, v_rows):
    for f in range(2):
        p = block * v_rows[f]
        p = p[:, :128] + p[:, 128:]
        acc[f] = p if acc[f] is None else acc[f] + p


def row_sums(parts):
    return jnp.sum(jnp.concatenate(parts, axis=0).T, axis=0, keepdims=True)


ROWS = 64


def apply_blocks(inner_ref, outer_ref, v_ref, obs_ref, y):
    for w in range(8):
        done = [[], []]
        for c in range(0, 256, ROWS):
            acc = [None, None]
            for shift in range(-W, W + 1):
                other = w + shift
                if 0 <= other < 8:
                    block = inner_ref[INNER.index((w, shift)), c : c + ROWS, :]
                else:
                    block = outer_ref[OUTER.index((w, shift)), c : c + ROWS, :]
                rows = [v_ref[f, other + W : other + W + 1, :] for f in range(2)]
                add_products(acc, block, rows)
            for f in range(2):
                done[f].append(acc[f])
        for f in range(2):
            y[f, w : w + 1, :] = row_sums(done[f]) + (obs_ref[w : w + 1, :] * SCALE) * v_ref[
                f, w + W : w + W + 1, :
            ]


def set_sends(even, p, a_ref, b_ref):
    for f in range(2):
        low, high = p[f, :W], p[f, W:]
        a_ref[f] = jnp.where(even, high, low)
        b_ref[f] = jnp.where(even, low, high)


def outer_kernel(
    reach_ref, own_ref, a_ref, b_ref, t_ref,
    outer_ref, p0_ref, obs_ref, field_a_ref, field_b_ref,
    xs, lines,
):
    even = lax.axis_index("space") % 2 == 0
    a_low, b_low = jnp.where(even, 0, 16), jnp.where(even, 16, 0)
    for w in range(8):
        xs[w + W] = tile_of(own_ref, 32 * w + (16 if w >= 4 else 0))
    for w in range(W):
        xs[jnp.where(even, 12, 0) + w] = tile_of(a_ref, pl.multiple_of(a_low + 32 * w, 16))
        xs[jnp.where(even, 0, 12) + w] = tile_of(b_ref, pl.multiple_of(b_low + 32 * w, 16))
    a_at = pl.multiple_of(jnp.where(even, 128, 0), 16)
    b_at = pl.multiple_of(jnp.where(even, 0, 128), 16)
    lines[0] = a_ref[:, pl.ds(a_at, 16), :]
    lines[1] = b_ref[:, pl.ds(b_at, 16), :]

    lane = lax.broadcasted_iota(jnp.int32, (1, 128), 1)
    reach_a = lines[0, 0, 9:10, :].astype(jnp.float32)
    reach_b = lines[1, 0, 9:10, :].astype(jnp.float32)
    reach_left = jnp.where(even, reach_b, reach_a)
    reach_right = jnp.where(even, reach_a, reach_b)

    def reach_of(tile):
        if 0 <= tile < 8:
            return reach_ref[tile]
        line, at = (reach_left, tile + 8) if tile < 0 else (reach_right, tile - 8)
        return jnp.sum(jnp.where(lane == at, line, 0.0)).astype(jnp.int32)

    reach = {tile: reach_of(tile) for tile in range(-W, 8 + W)}
    a_fields, b_fields = unpack_fields(lines[0]), unpack_fields(lines[1])
    own_fields = unpack_fields(own_ref[:, FIELDS : FIELDS + 16, :])
    for f in range(2):
        field_a_ref[f] = jnp.where(even, a_fields[f][:W], a_fields[f][W:])
        field_b_ref[f] = jnp.where(even, b_fields[f][W:], b_fields[f][:W])
        p0_ref[f] = own_fields[f]
    obs_ref[...] = own_fields[2]
    for w in range(8):
        rows = xs[w + W].T
        for shift in range(-W, W + 1):
            if (w, shift) not in OUTER:
                continue
            entry = table_entry(shift, reach[w], reach[w + shift])
            covariance = jnp.dot(rows, xs[w + shift + W], preferred_element_type=jnp.float32)
            outer_ref[OUTER.index((w, shift))] = covariance * t_ref[entry]


FIELD = jax.ShapeDtypeStruct((2, 8, 256), jnp.float32)
HALO = jax.ShapeDtypeStruct((2, W, 256), jnp.float32)


def outer_blocks(reach, own, a, b, table):
    return pl.pallas_call(
        outer_kernel,
        out_shape=(
            jax.ShapeDtypeStruct((len(OUTER), 256, 256), jnp.float32),
            FIELD,
            jax.ShapeDtypeStruct((8, 256), jnp.float32),
            HALO,
            HALO,
        ),
        in_specs=[SM] + [VM] * 4,
        out_specs=(VM,) * 5,
        scratch_shapes=[
            pltpu.VMEM((16, 256, 256), jnp.bfloat16),
            pltpu.VMEM((2, 16, 16, 128), jnp.bfloat16),
        ],
        compiler_params=params(22),
    )(reach, own, a, b, table)


def fill_window(even, p_ref, a_ref, b_ref, v):
    for f in range(2):
        v[f, :W] = jnp.where(even, b_ref[f], a_ref[f])
        v[f, W : W + 8] = p_ref[f]
        v[f, W + 8 :] = jnp.where(even, a_ref[f], b_ref[f])


def next_kernel(
    p_ref, a_ref, b_ref, obs_ref, inner_ref, outer_ref, y_ref, send_a_ref, send_b_ref, v
):
    even = lax.axis_index("space") % 2 == 0
    fill_window(even, p_ref, a_ref, b_ref, v)
    apply_blocks(inner_ref, outer_ref, v, obs_ref, y_ref)
    set_sends(even, y_ref, send_a_ref, send_b_ref)


def next_application(p, a, b, obs, inner, outer):
    return pl.pallas_call(
        next_kernel,
        out_shape=(FIELD, HALO, HALO),
        in_specs=[VM] * 6,
        out_specs=(VM,) * 3,
        scratch_shapes=[pltpu.VMEM((2, 16, 256), jnp.float32)],
        compiler_params=params(24),
    )(p, a, b, obs, inner, outer)


def two_sum(a, b):
    s = a + b
    t = s - a
    return s, (a - (s - t)) + (b - t)


def halves(a):
    c = a * 4097.0
    high = c - (c - a)
    return high, a - high


def two_product(a, b):
    p = a * b
    ah, al = halves(a)
    bh, bl = halves(b)
    return p, ((ah * bh - p) + ah * bl + al * bh) + al * bl


def pair_add(x, y):
    s, e = two_sum(x[0], y[0])
    e = e + (x[1] + y[1])
    high = s + e
    return high, e - (high - s)


def pair_times(x, y):
    p, e = two_product(x[0], y[0])
    return p, e + (x[0] * y[1] + x[1] * y[0])


def last_kernel(
    p_ref, a_ref, b_ref, obs_ref, inner_ref, outer_ref, p0_ref, p1_ref, y_ref, m_ref, v
):
    even = lax.axis_index("space") % 2 == 0
    fill_window(even, p_ref, a_ref, b_ref, v)
    apply_blocks(inner_ref, outer_ref, v, obs_ref, y_ref)
    powers = [p0_ref, p1_ref, p_ref, y_ref]
    row = lax.broadcasted_iota(jnp.int32, (8, 128), 0)
    lane = lax.broadcasted_iota(jnp.int32, (8, 128), 1)
    sums = []
    for f in range(2):
        packed = [jnp.zeros((8, 128), jnp.float32)] * 2
        for k in range(2 * ITERS):
            p, e = two_product(powers[k // 2][f], powers[(k + 1) // 2][f])
            total = pair_add((p[:, :128], e[:, :128]), (p[:, 128:], e[:, 128:]))
            for shift in (4, 2, 1):
                total = pair_add(total, [pltpu.roll(x, shift, 0) for x in total])
            packed = [jnp.where(row == k, x, y) for x, y in zip(total, packed)]
        for shift in (64, 32, 16, 8, 4, 2, 1):
            packed = pair_add(packed, [pltpu.roll(x, shift, 1) for x in packed])
        sums.append(packed)
    high = jnp.where(lane < 32, sums[0][0], sums[1][0])
    low = jnp.where(lane < 96, sums[0][1], sums[1][1])
    out = jnp.where(lane < 64, high, low)
    for k in range(32):
        m_ref[k] = out


def last_application(p, a, b, obs, inner, outer, p0, p1):
    return pl.pallas_call(
        last_kernel,
        out_shape=(FIELD, jax.ShapeDtypeStruct((32, 8, 128), jnp.float32)),
        in_specs=[VM] * 8,
        out_specs=(VM,) * 2,
        scratch_shapes=[pltpu.VMEM((2, 16, 256), jnp.float32)],
        compiler_params=params(24),
    )(p, a, b, obs, inner, outer, p0, p1)


def square_dot(poly, moment):
    total = None
    for k in range(2 * len(poly) - 1):
        coefficient = None
        for i in range(len(poly)):
            j = k - i
            if i > j or j >= len(poly):
                continue
            term = two_product(poly[i], poly[j])
            if i != j:
                term = (2.0 * term[0], 2.0 * term[1])
            coefficient = term if coefficient is None else pair_add(coefficient, term)
        term = pair_times(coefficient, moment[k])
        total = term if total is None else pair_add(total, term)
    return total[0] + total[1]


def finish_kernel(m_ref, p0_ref, p1_ref, p2_ref, p3_ref, inc_ref, res_ref):
    member = lax.axis_index("member")
    s = m_ref[0]
    e = jnp.zeros((8, 128), jnp.float32)
    for k in range(1, 32):
        s, t = two_sum(s, m_ref[k])
        e = e + t
    low = e + pltpu.roll(s, 64, 1)
    moment = [(s[k : k + 1], low[k : k + 1]) for k in range(2 * ITERS)]
    one = jnp.ones((1, 128), jnp.float32)
    residual, direction, increment = [one], [one], []
    norm_now = moment[0][0] + moment[0][1]
    for iteration in range(ITERS):
        step = norm_now / square_dot(direction, moment[1:])
        moved = [step * c for c in direction]
        increment = [x + y for x, y in zip(increment, moved)] + moved[len(increment) :]
        residual = residual[:1] + [
            (residual[i + 1] if i + 1 < len(residual) else 0.0) - c for i, c in enumerate(moved)
        ]
        if iteration + 1 < ITERS:
            norm_next = square_dot(residual, moment)
            ratio = norm_next / (norm_now + EPSILON)
            grown = [ratio * c for c in direction]
            direction = [x + y for x, y in zip(residual, grown)] + residual[len(grown) :]
            norm_now = norm_next
    shift = (128 - (member % 8) * 16) % 128
    upper = member >= 8
    powers = [p0_ref, p1_ref, p2_ref, p3_ref]
    for f in range(2):
        at = 32 * f
        mine = [
            pltpu.roll(jnp.where(upper, p[f, :, 128:], p[f, :, :128]), shift, 1) for p in powers
        ]
        inc = sum(c[:, at : at + 1] * x for c, x in zip(increment, mine)) * SCALE
        res = sum(c[:, at : at + 1] * x for c, x in zip(residual, mine))
        inc_ref[f] = inc[:, :16]
        res_ref[f] = res[:, :16]


def finish(m, p):
    shape = jax.ShapeDtypeStruct((2, 8, 16), jnp.float32)
    return pl.pallas_call(
        finish_kernel,
        out_shape=(shape, shape),
        in_specs=[VM] * 5,
        out_specs=(VM, VM),
        compiler_params=params(8),
    )(m, *p)


def on_device(anomalies, loc_blocks, tile_reach, obs_var, innovations):
    table = make_tables(loc_blocks)
    chunk = pack(anomalies, tile_reach, obs_var, innovations)
    own = lax.all_to_all(chunk, "member", 0, 0)
    odd = lax.axis_index("space") % 2
    to_a = lax.dynamic_slice_in_dim(own, 128 * (1 - odd), PART, 1)
    to_b = lax.dynamic_slice_in_dim(own, 128 * odd, PART, 1)
    a, b = pair_swap(to_a, 0), pair_swap(to_b, 1)
    inner = inner_blocks(tile_reach, own, table)
    outer, p0, obs, a, b = outer_blocks(tile_reach, own, a, b, table)
    p1, to_a, to_b = next_application(p0, a, b, obs, inner, outer)
    a, b = pair_swap(to_a, 0), pair_swap(to_b, 1)
    p2, to_a, to_b = next_application(p1, a, b, obs, inner, outer)
    a, b = pair_swap(to_a, 0), pair_swap(to_b, 1)
    p3, m = last_application(p2, a, b, obs, inner, outer, p0, p1)
    m = lax.all_to_all(m, "space", 0, 0)
    return finish(m, [p0, p1, p2, p3])


def solution(mesh):
    in_specs = (
        P("member", "space", None),
        P(),
        P("space"),
        P("space", "member"),
        P(None, "space", "member"),
    )
    out_specs = (P(None, "space", "member"), P(None, "space", "member"))
    return jax.shard_map(
        on_device, mesh=mesh, in_specs=in_specs, out_specs=out_specs, check_vma=False
    )
```

```python
import jax
import jax.numpy as jnp
from jax import lax
from jax.experimental import pallas as pl
from jax.experimental.pallas import tpu as pltpu
from jax.sharding import PartitionSpec as P

W = 4
ITERS = 3
EPSILON = 1e-6
SCALE = 2.0**-8
MIB = 1 << 20

VM = pl.BlockSpec(memory_space=pltpu.VMEM)
SM = pl.BlockSpec(memory_space=pltpu.SMEM)
HBM = pl.BlockSpec(memory_space=pltpu.HBM)

FIELDS = 128
PART = 144
CHUNK = 272

BASE = [0, 5, 9, 12, 14]
BASE_T = [0, 15, 19, 22, 24]
N_TABLE = 26

INNER = [(w, s) for w in range(8) for s in range(-W, W + 1) if 0 <= w + s < 8]
OUTER = [(w, s) for w in range(8) for s in range(-W, W + 1) if not 0 <= w + s < 8]


def params(mib):
    return pltpu.CompilerParams(vmem_limit_bytes=mib * MIB)


def pair_swap(block, offset):
    n, m = lax.axis_size("space"), lax.axis_size("member")
    route = []
    for i in range(n):
        j = i + 1 if (i + offset) % 2 == 0 else i - 1
        for k in range(m):
            route.append((i * m + k, (j % n) * m + (k if 0 <= j < n else k ^ 1)))
    return lax.ppermute(block, ("space", "member"), route)


def pack_kernel(
    anomalies_hbm, reach_hbm, obs_hbm, innovations_hbm, chunk_ref, x_ref, reach_ref, obs_ref, inn_ref, sems
):
    moves = [(anomalies_hbm, x_ref), (innovations_hbm, inn_ref), (obs_hbm, obs_ref), (reach_hbm, reach_ref)]
    copies = [pltpu.make_async_copy(x, y, sems.at[i]) for i, (x, y) in enumerate(moves)]
    for copy in copies:
        copy.start()
    for copy in copies:
        copy.wait()
    x = x_ref[...].astype(jnp.float32)
    rows = []
    for t in range(8):
        tile = x[:, t, :]
        rows += [tile[:, :128], tile[:, 128:]]
    lane = lax.broadcasted_iota(jnp.int32, (1, 128), 1)
    lines = []
    for a in range(3):
        block = inn_ref[a] if a < 2 else obs_ref[...]
        wide = jnp.concatenate([block, jnp.zeros((8, 112), jnp.float32)], axis=1)
        line = wide[0:1]
        for t in range(1, 8):
            line = line + pltpu.roll(wide[t : t + 1], 16 * t, 1)
        lines.append(line)
    values = jnp.concatenate(lines, axis=0)
    high = values.astype(jnp.bfloat16).astype(jnp.float32)
    rest = values - high
    middle = rest.astype(jnp.bfloat16).astype(jnp.float32)
    reach = jnp.zeros((1, 128), jnp.float32)
    for t in range(8):
        reach = reach + jnp.where(lane == t, reach_ref[t].astype(jnp.float32), 0.0)
    fields = jnp.concatenate(
        [high, middle, rest - middle, reach, jnp.zeros((6, 128), jnp.float32)], axis=0
    )
    chunk_ref[...] = jnp.concatenate(rows[:8] + [fields] + rows[8:], axis=0).astype(jnp.bfloat16)


def pack(anomalies, tile_reach, obs_var, innovations):
    return pl.pallas_call(
        pack_kernel,
        out_shape=jax.ShapeDtypeStruct((CHUNK, 128), jnp.bfloat16),
        in_specs=[HBM] * 4,
        out_specs=VM,
        scratch_shapes=[
            pltpu.VMEM(anomalies.shape, jnp.bfloat16),
            pltpu.SMEM((8,), jnp.int32),
            pltpu.VMEM(obs_var.shape, jnp.float32),
            pltpu.VMEM(innovations.shape, jnp.float32),
            pltpu.SemaphoreType.DMA((4,)),
        ],
        compiler_params=params(8),
    )(anomalies, tile_reach, obs_var, innovations)


def spread_kernel(mine_ref, other_ref, out_ref):
    y = lax.axis_index("member") % 2 == 0
    low = jnp.where(y, mine_ref[...], other_ref[...])
    high = jnp.where(y, other_ref[...], mine_ref[...])
    for k in range(8):
        out_ref[k, :CHUNK] = low
        out_ref[k, CHUNK:] = high


def gather_members(chunk):
    n, m = lax.axis_size("space"), lax.axis_size("member")
    other = lax.ppermute(chunk, "member", [(k, k ^ 1) for k in range(m)])
    both = pl.pallas_call(
        spread_kernel,
        out_shape=jax.ShapeDtypeStruct((8, 2 * CHUNK, 128), jnp.bfloat16),
        in_specs=[VM, VM],
        out_specs=VM,
        compiler_params=params(8),
    )(chunk, other)
    groups = [[2 * z + y for z in range(8)] for y in range(2)]
    out = lax.all_to_all(both, "member", 0, 0, axis_index_groups=groups)
    return out.reshape(16, CHUNK, 128)


def swap_blocks(x):
    row = lax.broadcasted_iota(jnp.int32, (8, 128), 0)
    block = lax.broadcasted_iota(jnp.int32, (8, 128), 1) // 16
    for bit in (1, 2, 4):
        r, b = (row & bit) != 0, (block & bit) != 0
        up = pltpu.roll(pltpu.roll(x, 8 - bit, 0), 16 * bit, 1)
        down = pltpu.roll(pltpu.roll(x, bit, 0), 128 - 16 * bit, 1)
        x = jnp.where(r == b, x, jnp.where(b, up, down))
    return x


def unpack_fields(lines):
    lines = lines.astype(jnp.float32)
    out = []
    for a in range(3):
        value = lines[:, a] + (lines[:, 3 + a] + lines[:, 6 + a])
        out.append(jnp.concatenate([swap_blocks(value[:8]), swap_blocks(value[8:])], axis=1))
    return out


def row_products(a, b):
    return lax.dot_general(a, b, (((1,), (1,)), ((), ())), preferred_element_type=jnp.float32)


def tile_of(ref, row):
    return jnp.concatenate(
        [
            ref[:, pl.ds(row, 16), :].reshape(256, 128),
            ref[:, pl.ds(row + 16, 16), :].reshape(256, 128),
        ],
        axis=1,
    )


def table_entry(shift, reach_w, reach_o):
    d = abs(shift)
    if shift >= 0:
        last, base = jnp.minimum(reach_o, reach_w - d), BASE[d]
    else:
        last, base = jnp.minimum(reach_w, reach_o - d), BASE_T[d]
    return jnp.where(last >= 0, base + last, N_TABLE - 1)


def table_kernel(loc_ref, t_ref):
    factor = SCALE / 255.0
    k = 0
    for d in range(W + 1):
        total = None
        for o in range(W + 1 - d):
            p = row_products(loc_ref[o + d], loc_ref[o])
            total = p if total is None else total + p
            t_ref[k] = total * factor
            k += 1
    for d in range(1, W + 1):
        total = None
        for o in range(W + 1 - d):
            p = row_products(loc_ref[o], loc_ref[o + d])
            total = p if total is None else total + p
            t_ref[k] = total * factor
            k += 1
    t_ref[k] = jnp.zeros(t_ref.shape[1:], jnp.float32)


def make_tables(loc_blocks):
    return pl.pallas_call(
        table_kernel,
        out_shape=jax.ShapeDtypeStruct((N_TABLE, 256, 256), jnp.float32),
        in_specs=[VM],
        out_specs=VM,
        compiler_params=params(14),
        cost_estimate=pl.CostEstimate(
            flops=25 * 2 * 256**3, bytes_accessed=7 * MIB, transcendentals=0
        ),
    )(loc_blocks)


FIELD = jax.ShapeDtypeStruct((2, 8, 256), jnp.float32)
HALO = jax.ShapeDtypeStruct((2, W, 256), jnp.float32)
ROWS = 64


def apply_blocks(pairs, block_ref, field_row):
    out = []
    for w in range(8):
        mine = [(k, w + shift) for k, (row, shift) in enumerate(pairs) if row == w]
        done = [[], []]
        for c in range(0, 256, ROWS):
            acc = [None, None]
            for k, other in mine:
                block = block_ref[k, c : c + ROWS, :]
                for f in range(2):
                    p = block * field_row(f, other)
                    p = p[:, :128] + p[:, 128:]
                    acc[f] = p if acc[f] is None else acc[f] + p
            for f in range(2):
                done[f].append(acc[f])
        for f in range(2):
            total = jnp.sum(jnp.concatenate(done[f], axis=0).T, axis=0, keepdims=True)
            out.append((f, w, total))
    return out


def apply_inner(inner_ref, p_ref, obs_ref, part_ref):
    for f, w, total in apply_blocks(INNER, inner_ref, lambda f, t: p_ref[f, t : t + 1, :]):
        own = (obs_ref[w : w + 1, :] * SCALE) * p_ref[f, w : w + 1, :]
        part_ref[f, w : w + 1, :] = total + own


def apply_outer(outer_ref, part_ref, halo, y_ref):
    def row(f, t):
        at = t + W if t < 0 else t - W
        return halo[f, at : at + 1, :]

    for f, w, total in apply_blocks(OUTER, outer_ref, row):
        y_ref[f, w : w + 1, :] = total + part_ref[f, w : w + 1, :]


def inner_kernel(reach_ref, own_ref, t_ref, h_ref, p0_ref, obs_ref, part_ref, xs):
    for w in range(8):
        xs[w] = tile_of(own_ref, 32 * w + (16 if w >= 4 else 0))
    fields = unpack_fields(own_ref[:, FIELDS : FIELDS + 16, :])
    for f in range(2):
        p0_ref[f] = fields[f]
    obs_ref[...] = fields[2]
    for w in range(8):
        rows = xs[w].T
        for shift in range(-W, W + 1):
            if (w, shift) not in INNER:
                continue
            entry = table_entry(shift, reach_ref[w], reach_ref[w + shift])
            covariance = jnp.dot(rows, xs[w + shift], preferred_element_type=jnp.float32)
            h_ref[INNER.index((w, shift))] = covariance * t_ref[entry]
    apply_inner(h_ref, p0_ref, obs_ref, part_ref)


def inner_blocks(reach, own, table):
    return pl.pallas_call(
        inner_kernel,
        out_shape=(
            jax.ShapeDtypeStruct((len(INNER), 256, 256), jnp.float32),
            FIELD,
            jax.ShapeDtypeStruct((8, 256), jnp.float32),
            FIELD,
        ),
        in_specs=[SM, VM, VM],
        out_specs=(VM,) * 4,
        scratch_shapes=[pltpu.VMEM((8, 256, 256), jnp.bfloat16)],
        compiler_params=params(26),
        cost_estimate=pl.CostEstimate(
            flops=100 * 2 * 256**3, bytes_accessed=20 * MIB, transcendentals=0
        ),
    )(reach, own, table)


def set_sends(even, p, a_ref, b_ref):
    for f in range(2):
        low, high = p[f, :W], p[f, W:]
        a_ref[f] = jnp.where(even, high, low)
        b_ref[f] = jnp.where(even, low, high)


def fill_halo(even, a, b, halo):
    for f in range(2):
        halo[f, :W] = jnp.where(even, b[f], a[f])
        halo[f, W:] = jnp.where(even, a[f], b[f])


def outer_kernel(
    reach_ref, own_ref, a_ref, b_ref, t_ref, part_ref,
    outer_ref, y_ref, send_a_ref, send_b_ref,
    xs, lines, halo,
):
    even = lax.axis_index("space") % 2 == 0
    a_low, b_low = jnp.where(even, 0, 16), jnp.where(even, 16, 0)
    for w in range(8):
        xs[w + W] = tile_of(own_ref, 32 * w + (16 if w >= 4 else 0))
    for w in range(W):
        xs[jnp.where(even, 12, 0) + w] = tile_of(a_ref, pl.multiple_of(a_low + 32 * w, 16))
        xs[jnp.where(even, 0, 12) + w] = tile_of(b_ref, pl.multiple_of(b_low + 32 * w, 16))
    a_at = pl.multiple_of(jnp.where(even, 128, 0), 16)
    b_at = pl.multiple_of(jnp.where(even, 0, 128), 16)
    lines[0] = a_ref[:, pl.ds(a_at, 16), :]
    lines[1] = b_ref[:, pl.ds(b_at, 16), :]

    lane = lax.broadcasted_iota(jnp.int32, (1, 128), 1)
    reach_a = lines[0, 0, 9:10, :].astype(jnp.float32)
    reach_b = lines[1, 0, 9:10, :].astype(jnp.float32)
    reach_left = jnp.where(even, reach_b, reach_a)
    reach_right = jnp.where(even, reach_a, reach_b)

    def reach_of(tile):
        if 0 <= tile < 8:
            return reach_ref[tile]
        line, at = (reach_left, tile + 8) if tile < 0 else (reach_right, tile - 8)
        return jnp.sum(jnp.where(lane == at, line, 0.0)).astype(jnp.int32)

    reach = {tile: reach_of(tile) for tile in range(-W, 8 + W)}
    a_fields, b_fields = unpack_fields(lines[0]), unpack_fields(lines[1])
    fill_halo(
        even,
        [jnp.where(even, x[:W], x[W:]) for x in a_fields[:2]],
        [jnp.where(even, x[W:], x[:W]) for x in b_fields[:2]],
        halo,
    )
    for w in range(8):
        rows = xs[w + W].T
        for shift in range(-W, W + 1):
            if (w, shift) not in OUTER:
                continue
            entry = table_entry(shift, reach[w], reach[w + shift])
            covariance = jnp.dot(rows, xs[w + shift + W], preferred_element_type=jnp.float32)
            outer_ref[OUTER.index((w, shift))] = covariance * t_ref[entry]
    apply_outer(outer_ref, part_ref, halo, y_ref)
    set_sends(even, y_ref, send_a_ref, send_b_ref)


def outer_blocks(reach, own, a, b, table, part):
    return pl.pallas_call(
        outer_kernel,
        out_shape=(
            jax.ShapeDtypeStruct((len(OUTER), 256, 256), jnp.float32),
            FIELD,
            HALO,
            HALO,
        ),
        in_specs=[SM] + [VM] * 5,
        out_specs=(VM,) * 4,
        scratch_shapes=[
            pltpu.VMEM((16, 256, 256), jnp.bfloat16),
            pltpu.VMEM((2, 16, 16, 128), jnp.bfloat16),
            pltpu.VMEM((2, 8, 256), jnp.float32),
        ],
        compiler_params=params(22),
    )(reach, own, a, b, table, part)


def next_inner(p, obs, inner):
    return pl.pallas_call(
        lambda p_ref, obs_ref, inner_ref, part_ref: apply_inner(inner_ref, p_ref, obs_ref, part_ref),
        out_shape=FIELD,
        in_specs=[VM] * 3,
        out_specs=VM,
        compiler_params=params(18),
        cost_estimate=pl.CostEstimate(
            flops=50 * 2 * 256**3, bytes_accessed=14 * MIB, transcendentals=0
        ),
    )(p, obs, inner)


def next_kernel(part_ref, a_ref, b_ref, outer_ref, y_ref, send_a_ref, send_b_ref, halo):
    even = lax.axis_index("space") % 2 == 0
    fill_halo(even, a_ref, b_ref, halo)
    apply_outer(outer_ref, part_ref, halo, y_ref)
    set_sends(even, y_ref, send_a_ref, send_b_ref)


def next_outer(part, a, b, outer):
    return pl.pallas_call(
        next_kernel,
        out_shape=(FIELD, HALO, HALO),
        in_specs=[VM] * 4,
        out_specs=(VM,) * 3,
        scratch_shapes=[pltpu.VMEM((2, 8, 256), jnp.float32)],
        compiler_params=params(10),
    )(part, a, b, outer)


def two_sum(a, b):
    s = a + b
    t = s - a
    return s, (a - (s - t)) + (b - t)


def halves(a):
    c = a * 4097.0
    high = c - (c - a)
    return high, a - high


def two_product(a, b):
    p = a * b
    ah, al = halves(a)
    bh, bl = halves(b)
    return p, ((ah * bh - p) + ah * bl + al * bh) + al * bl


def pair_add(x, y):
    s, e = two_sum(x[0], y[0])
    e = e + (x[1] + y[1])
    high = s + e
    return high, e - (high - s)


def pair_times(x, y):
    p, e = two_product(x[0], y[0])
    return p, e + (x[0] * y[1] + x[1] * y[0])


def last_kernel(part_ref, a_ref, b_ref, outer_ref, p0_ref, p1_ref, p2_ref, y_ref, m_ref, halo):
    even = lax.axis_index("space") % 2 == 0
    fill_halo(even, a_ref, b_ref, halo)
    apply_outer(outer_ref, part_ref, halo, y_ref)
    powers = [p0_ref, p1_ref, p2_ref, y_ref]
    row = lax.broadcasted_iota(jnp.int32, (8, 128), 0)
    lane = lax.broadcasted_iota(jnp.int32, (8, 128), 1)
    sums = []
    for f in range(2):
        packed = [jnp.zeros((8, 128), jnp.float32)] * 2
        for k in range(2 * ITERS):
            p, e = two_product(powers[k // 2][f], powers[(k + 1) // 2][f])
            total = pair_add((p[:, :128], e[:, :128]), (p[:, 128:], e[:, 128:]))
            for shift in (4, 2, 1):
                total = pair_add(total, [pltpu.roll(x, shift, 0) for x in total])
            packed = [jnp.where(row == k, x, y) for x, y in zip(total, packed)]
        for shift in (64, 32, 16, 8, 4, 2, 1):
            packed = pair_add(packed, [pltpu.roll(x, shift, 1) for x in packed])
        sums.append(packed)
    high = jnp.where(lane < 32, sums[0][0], sums[1][0])
    low = jnp.where(lane < 96, sums[0][1], sums[1][1])
    out = jnp.where(lane < 64, high, low)
    for k in range(32):
        m_ref[k] = out


def last_outer(part, a, b, outer, p0, p1, p2):
    return pl.pallas_call(
        last_kernel,
        out_shape=(FIELD, jax.ShapeDtypeStruct((32, 8, 128), jnp.float32)),
        in_specs=[VM] * 7,
        out_specs=(VM,) * 2,
        scratch_shapes=[pltpu.VMEM((2, 8, 256), jnp.float32)],
        compiler_params=params(10),
    )(part, a, b, outer, p0, p1, p2)


def square_dot(poly, moment):
    total = None
    for k in range(2 * len(poly) - 1):
        coefficient = None
        for i in range(len(poly)):
            j = k - i
            if i > j or j >= len(poly):
                continue
            term = two_product(poly[i], poly[j])
            if i != j:
                term = (2.0 * term[0], 2.0 * term[1])
            coefficient = term if coefficient is None else pair_add(coefficient, term)
        term = pair_times(coefficient, moment[k])
        total = term if total is None else pair_add(total, term)
    return total[0] + total[1]


def finish_kernel(m_ref, p0_ref, p1_ref, p2_ref, p3_ref, inc_ref, res_ref):
    member = lax.axis_index("member")
    s = m_ref[0]
    e = jnp.zeros((8, 128), jnp.float32)
    for k in range(1, 32):
        s, t = two_sum(s, m_ref[k])
        e = e + t
    low = e + pltpu.roll(s, 64, 1)
    moment = [(s[k : k + 1], low[k : k + 1]) for k in range(2 * ITERS)]
    one = jnp.ones((1, 128), jnp.float32)
    residual, direction, increment = [one], [one], []
    norm_now = moment[0][0] + moment[0][1]
    for iteration in range(ITERS):
        step = norm_now / square_dot(direction, moment[1:])
        moved = [step * c for c in direction]
        increment = [x + y for x, y in zip(increment, moved)] + moved[len(increment) :]
        residual = residual[:1] + [
            (residual[i + 1] if i + 1 < len(residual) else 0.0) - c for i, c in enumerate(moved)
        ]
        if iteration + 1 < ITERS:
            norm_next = square_dot(residual, moment)
            ratio = norm_next / (norm_now + EPSILON)
            grown = [ratio * c for c in direction]
            direction = [x + y for x, y in zip(residual, grown)] + residual[len(grown) :]
            norm_now = norm_next
    shift = (128 - (member % 8) * 16) % 128
    upper = member >= 8
    powers = [p0_ref, p1_ref, p2_ref, p3_ref]
    for f in range(2):
        at = 32 * f
        mine = [
            pltpu.roll(jnp.where(upper, p[f, :, 128:], p[f, :, :128]), shift, 1) for p in powers
        ]
        inc = sum(c[:, at : at + 1] * x for c, x in zip(increment, mine)) * SCALE
        res = sum(c[:, at : at + 1] * x for c, x in zip(residual, mine))
        inc_ref[f] = inc[:, :16]
        res_ref[f] = res[:, :16]


def finish(m, p):
    shape = jax.ShapeDtypeStruct((2, 8, 16), jnp.float32)
    return pl.pallas_call(
        finish_kernel,
        out_shape=(shape, shape),
        in_specs=[VM] * 5,
        out_specs=(VM, VM),
        compiler_params=params(8),
    )(m, *p)


def on_device(anomalies, loc_blocks, tile_reach, obs_var, innovations):
    table = make_tables(loc_blocks)
    own = gather_members(pack(anomalies, tile_reach, obs_var, innovations))
    odd = lax.axis_index("space") % 2
    to_a = lax.dynamic_slice_in_dim(own, 128 * (1 - odd), PART, 1)
    to_b = lax.dynamic_slice_in_dim(own, 128 * odd, PART, 1)
    a, b = pair_swap(to_a, 0), pair_swap(to_b, 1)
    inner, p0, obs, part = inner_blocks(tile_reach, own, table)
    outer, p1, to_a, to_b = outer_blocks(tile_reach, own, a, b, table, part)
    a, b = pair_swap(to_a, 0), pair_swap(to_b, 1)
    part = next_inner(p1, obs, inner)
    p2, to_a, to_b = next_outer(part, a, b, outer)
    a, b = pair_swap(to_a, 0), pair_swap(to_b, 1)
    part = next_inner(p2, obs, inner)
    p3, m = last_outer(part, a, b, outer, p0, p1, p2)
    m = lax.all_to_all(m, "space", 0, 0)
    return finish(m, [p0, p1, p2, p3])


def solution(mesh):
    in_specs = (
        P("member", "space", None),
        P(),
        P("space"),
        P("space", "member"),
        P(None, "space", "member"),
    )
    out_specs = (P(None, "space", "member"), P(None, "space", "member"))
    return jax.shard_map(
        on_device, mesh=mesh, in_specs=in_specs, out_specs=out_specs, check_vma=False
    )
```

```python
import jax
import jax.numpy as jnp
from jax import lax
from jax.experimental import pallas as pl
from jax.experimental.pallas import tpu as pltpu
from jax.sharding import PartitionSpec as P

W = 4
ITERS = 3
EPSILON = 1e-6
SCALE = 2.0**-8
MIB = 1 << 20
PACK_MIB = 63

VM = pl.BlockSpec(memory_space=pltpu.VMEM)
SM = pl.BlockSpec(memory_space=pltpu.SMEM)
HBM = pl.BlockSpec(memory_space=pltpu.HBM)

FIELDS = 128
PART = 144
CHUNK = 272

BASE = [0, 5, 9, 12, 14]
BASE_T = [0, 15, 19, 22, 24]
N_TABLE = 26

INNER = [(w, s) for w in range(8) for s in range(-W, W + 1) if 0 <= w + s < 8]
OUTER = [(w, s) for w in range(8) for s in range(-W, W + 1) if not 0 <= w + s < 8]


def params(mib):
    return pltpu.CompilerParams(vmem_limit_bytes=mib * MIB)


def pair_swap(block, offset):
    n, m = lax.axis_size("space"), lax.axis_size("member")
    route = []
    for i in range(n):
        j = i + 1 if (i + offset) % 2 == 0 else i - 1
        for k in range(m):
            route.append((i * m + k, (j % n) * m + (k if 0 <= j < n else k ^ 1)))
    return lax.ppermute(block, ("space", "member"), route)


def pack_kernel(
    anomalies_hbm, reach_hbm, obs_hbm, innovations_hbm, chunk_ref, x_ref, reach_ref, obs_ref, inn_ref, sems
):
    moves = [(anomalies_hbm, x_ref), (innovations_hbm, inn_ref), (obs_hbm, obs_ref), (reach_hbm, reach_ref)]
    copies = [pltpu.make_async_copy(x, y, sems.at[i]) for i, (x, y) in enumerate(moves)]
    for copy in copies:
        copy.start()
    for copy in copies:
        copy.wait()
    x = x_ref[...].astype(jnp.float32)
    rows = []
    for t in range(8):
        tile = x[:, t, :]
        rows += [tile[:, :128], tile[:, 128:]]
    lane = lax.broadcasted_iota(jnp.int32, (1, 128), 1)
    lines = []
    for a in range(3):
        block = inn_ref[a] if a < 2 else obs_ref[...]
        wide = jnp.concatenate([block, jnp.zeros((8, 112), jnp.float32)], axis=1)
        line = wide[0:1]
        for t in range(1, 8):
            line = line + pltpu.roll(wide[t : t + 1], 16 * t, 1)
        lines.append(line)
    values = jnp.concatenate(lines, axis=0)
    high = values.astype(jnp.bfloat16).astype(jnp.float32)
    rest = values - high
    middle = rest.astype(jnp.bfloat16).astype(jnp.float32)
    reach = jnp.zeros((1, 128), jnp.float32)
    for t in range(8):
        reach = reach + jnp.where(lane == t, reach_ref[t].astype(jnp.float32), 0.0)
    fields = jnp.concatenate(
        [high, middle, rest - middle, reach, jnp.zeros((6, 128), jnp.float32)], axis=0
    )
    chunk_ref[...] = jnp.concatenate(rows[:8] + [fields] + rows[8:], axis=0).astype(jnp.bfloat16)


def pack(anomalies, tile_reach, obs_var, innovations):
    return pl.pallas_call(
        pack_kernel,
        out_shape=jax.ShapeDtypeStruct((CHUNK, 128), jnp.bfloat16),
        in_specs=[HBM] * 4,
        out_specs=VM,
        scratch_shapes=[
            pltpu.VMEM(anomalies.shape, jnp.bfloat16),
            pltpu.SMEM((8,), jnp.int32),
            pltpu.VMEM(obs_var.shape, jnp.float32),
            pltpu.VMEM(innovations.shape, jnp.float32),
            pltpu.SemaphoreType.DMA((4,)),
        ],
        compiler_params=params(PACK_MIB),
    )(anomalies, tile_reach, obs_var, innovations)


def spread_kernel(mine_ref, other_ref, out_ref):
    y = lax.axis_index("member") % 2 == 0
    low = jnp.where(y, mine_ref[...], other_ref[...])
    high = jnp.where(y, other_ref[...], mine_ref[...])
    for k in range(8):
        out_ref[k, :CHUNK] = low
        out_ref[k, CHUNK:] = high


def gather_members(chunk):
    n, m = lax.axis_size("space"), lax.axis_size("member")
    other = lax.ppermute(chunk, "member", [(k, k ^ 1) for k in range(m)])
    both = pl.pallas_call(
        spread_kernel,
        out_shape=jax.ShapeDtypeStruct((8, 2 * CHUNK, 128), jnp.bfloat16),
        in_specs=[VM, VM],
        out_specs=VM,
        compiler_params=params(8),
    )(chunk, other)
    groups = [[2 * z + y for z in range(8)] for y in range(2)]
    out = lax.all_to_all(both, "member", 0, 0, axis_index_groups=groups)
    return out.reshape(16, CHUNK, 128)


def swap_blocks(x):
    row = lax.broadcasted_iota(jnp.int32, (8, 128), 0)
    block = lax.broadcasted_iota(jnp.int32, (8, 128), 1) // 16
    for bit in (1, 2, 4):
        r, b = (row & bit) != 0, (block & bit) != 0
        up = pltpu.roll(pltpu.roll(x, 8 - bit, 0), 16 * bit, 1)
        down = pltpu.roll(pltpu.roll(x, bit, 0), 128 - 16 * bit, 1)
        x = jnp.where(r == b, x, jnp.where(b, up, down))
    return x


def unpack_fields(lines):
    lines = lines.astype(jnp.float32)
    out = []
    for a in range(3):
        value = lines[:, a] + (lines[:, 3 + a] + lines[:, 6 + a])
        out.append(jnp.concatenate([swap_blocks(value[:8]), swap_blocks(value[8:])], axis=1))
    return out


def row_products(a, b):
    return lax.dot_general(a, b, (((1,), (1,)), ((), ())), preferred_element_type=jnp.float32)


def tile_of(ref, row):
    return jnp.concatenate(
        [
            ref[:, pl.ds(row, 16), :].reshape(256, 128),
            ref[:, pl.ds(row + 16, 16), :].reshape(256, 128),
        ],
        axis=1,
    )


def table_entry(shift, reach_w, reach_o):
    d = abs(shift)
    if shift >= 0:
        last, base = jnp.minimum(reach_o, reach_w - d), BASE[d]
    else:
        last, base = jnp.minimum(reach_w, reach_o - d), BASE_T[d]
    return jnp.where(last >= 0, base + last, N_TABLE - 1)


def fill_table(loc_ref, t_ref):
    factor = SCALE / 255.0
    k = 0
    for d in range(W + 1):
        total = None
        for o in range(W + 1 - d):
            p = row_products(loc_ref[o + d], loc_ref[o])
            total = p if total is None else total + p
            t_ref[k] = total * factor
            k += 1
    for d in range(1, W + 1):
        total = None
        for o in range(W + 1 - d):
            p = row_products(loc_ref[o], loc_ref[o + d])
            total = p if total is None else total + p
            t_ref[k] = total * factor
            k += 1
    t_ref[k] = jnp.zeros(t_ref.shape[1:], jnp.float32)


FIELD = jax.ShapeDtypeStruct((2, 8, 256), jnp.float32)
HALO = jax.ShapeDtypeStruct((2, W, 256), jnp.float32)
ROWS = 64


def apply_blocks(pairs, block_ref, field_row):
    out = []
    for w in range(8):
        mine = [(k, w + shift) for k, (row, shift) in enumerate(pairs) if row == w]
        done = [[], []]
        for c in range(0, 256, ROWS):
            acc = [None, None]
            for k, other in mine:
                block = block_ref[k, c : c + ROWS, :]
                for f in range(2):
                    p = block * field_row(f, other)
                    p = p[:, :128] + p[:, 128:]
                    acc[f] = p if acc[f] is None else acc[f] + p
            for f in range(2):
                done[f].append(acc[f])
        for f in range(2):
            total = jnp.sum(jnp.concatenate(done[f], axis=0).T, axis=0, keepdims=True)
            out.append((f, w, total))
    return out


def apply_inner(inner_ref, p_ref, obs_ref, part_ref):
    for f, w, total in apply_blocks(INNER, inner_ref, lambda f, t: p_ref[f, t : t + 1, :]):
        own = (obs_ref[w : w + 1, :] * SCALE) * p_ref[f, w : w + 1, :]
        part_ref[f, w : w + 1, :] = total + own


def apply_outer(outer_ref, part_ref, halo, y_ref):
    def row(f, t):
        at = t + W if t < 0 else t - W
        return halo[f, at : at + 1, :]

    for f, w, total in apply_blocks(OUTER, outer_ref, row):
        y_ref[f, w : w + 1, :] = total + part_ref[f, w : w + 1, :]


def inner_kernel(reach_ref, loc_ref, own_ref, t_ref, h_ref, p0_ref, obs_ref, part_ref, xs):
    fill_table(loc_ref, t_ref)
    for w in range(8):
        xs[w] = tile_of(own_ref, 32 * w + (16 if w >= 4 else 0))
    fields = unpack_fields(own_ref[:, FIELDS : FIELDS + 16, :])
    for f in range(2):
        p0_ref[f] = fields[f]
    obs_ref[...] = fields[2]
    for w in range(8):
        rows = xs[w].T
        for shift in range(-W, W + 1):
            if (w, shift) not in INNER:
                continue
            entry = table_entry(shift, reach_ref[w], reach_ref[w + shift])
            covariance = jnp.dot(rows, xs[w + shift], preferred_element_type=jnp.float32)
            h_ref[INNER.index((w, shift))] = covariance * t_ref[entry]
    apply_inner(h_ref, p0_ref, obs_ref, part_ref)


def inner_blocks(reach, loc_blocks, own):
    return pl.pallas_call(
        inner_kernel,
        out_shape=(
            jax.ShapeDtypeStruct((N_TABLE, 256, 256), jnp.float32),
            jax.ShapeDtypeStruct((len(INNER), 256, 256), jnp.float32),
            FIELD,
            jax.ShapeDtypeStruct((8, 256), jnp.float32),
            FIELD,
        ),
        in_specs=[SM, VM, VM],
        out_specs=(VM,) * 5,
        scratch_shapes=[pltpu.VMEM((8, 256, 256), jnp.bfloat16)],
        compiler_params=params(12),
        cost_estimate=pl.CostEstimate(
            flops=100 * 2 * 256**3, bytes_accessed=20 * MIB, transcendentals=0
        ),
    )(reach, loc_blocks, own)


def set_sends(even, p, a_ref, b_ref):
    for f in range(2):
        low, high = p[f, :W], p[f, W:]
        a_ref[f] = jnp.where(even, high, low)
        b_ref[f] = jnp.where(even, low, high)


def fill_halo(even, a, b, halo):
    for f in range(2):
        halo[f, :W] = jnp.where(even, b[f], a[f])
        halo[f, W:] = jnp.where(even, a[f], b[f])


def outer_kernel(
    reach_ref, own_ref, a_ref, b_ref, t_ref, part_ref,
    outer_ref, y_ref, send_a_ref, send_b_ref,
    xs, lines, halo,
):
    even = lax.axis_index("space") % 2 == 0
    a_low, b_low = jnp.where(even, 0, 16), jnp.where(even, 16, 0)
    for w in range(8):
        xs[w + W] = tile_of(own_ref, 32 * w + (16 if w >= 4 else 0))
    for w in range(W):
        xs[jnp.where(even, 12, 0) + w] = tile_of(a_ref, pl.multiple_of(a_low + 32 * w, 16))
        xs[jnp.where(even, 0, 12) + w] = tile_of(b_ref, pl.multiple_of(b_low + 32 * w, 16))
    a_at = pl.multiple_of(jnp.where(even, 128, 0), 16)
    b_at = pl.multiple_of(jnp.where(even, 0, 128), 16)
    lines[0] = a_ref[:, pl.ds(a_at, 16), :]
    lines[1] = b_ref[:, pl.ds(b_at, 16), :]

    lane = lax.broadcasted_iota(jnp.int32, (1, 128), 1)
    reach_a = lines[0, 0, 9:10, :].astype(jnp.float32)
    reach_b = lines[1, 0, 9:10, :].astype(jnp.float32)
    reach_left = jnp.where(even, reach_b, reach_a)
    reach_right = jnp.where(even, reach_a, reach_b)

    def reach_of(tile):
        if 0 <= tile < 8:
            return reach_ref[tile]
        line, at = (reach_left, tile + 8) if tile < 0 else (reach_right, tile - 8)
        return jnp.sum(jnp.where(lane == at, line, 0.0)).astype(jnp.int32)

    reach = {tile: reach_of(tile) for tile in range(-W, 8 + W)}
    a_fields, b_fields = unpack_fields(lines[0]), unpack_fields(lines[1])
    fill_halo(
        even,
        [jnp.where(even, x[:W], x[W:]) for x in a_fields[:2]],
        [jnp.where(even, x[W:], x[:W]) for x in b_fields[:2]],
        halo,
    )
    for w in range(8):
        rows = xs[w + W].T
        for shift in range(-W, W + 1):
            if (w, shift) not in OUTER:
                continue
            entry = table_entry(shift, reach[w], reach[w + shift])
            covariance = jnp.dot(rows, xs[w + shift + W], preferred_element_type=jnp.float32)
            outer_ref[OUTER.index((w, shift))] = covariance * t_ref[entry]
    apply_outer(outer_ref, part_ref, halo, y_ref)
    set_sends(even, y_ref, send_a_ref, send_b_ref)


def outer_blocks(reach, own, a, b, table, part):
    return pl.pallas_call(
        outer_kernel,
        out_shape=(
            jax.ShapeDtypeStruct((len(OUTER), 256, 256), jnp.float32),
            FIELD,
            HALO,
            HALO,
        ),
        in_specs=[SM] + [VM] * 5,
        out_specs=(VM,) * 4,
        scratch_shapes=[
            pltpu.VMEM((16, 256, 256), jnp.bfloat16),
            pltpu.VMEM((2, 16, 16, 128), jnp.bfloat16),
            pltpu.VMEM((2, 8, 256), jnp.float32),
        ],
        compiler_params=params(12),
    )(reach, own, a, b, table, part)


def next_inner(p, obs, inner):
    return pl.pallas_call(
        lambda p_ref, obs_ref, inner_ref, part_ref: apply_inner(inner_ref, p_ref, obs_ref, part_ref),
        out_shape=FIELD,
        in_specs=[VM] * 3,
        out_specs=VM,
        compiler_params=params(6),
        cost_estimate=pl.CostEstimate(
            flops=50 * 2 * 256**3, bytes_accessed=14 * MIB, transcendentals=0
        ),
    )(p, obs, inner)


def next_kernel(part_ref, a_ref, b_ref, outer_ref, y_ref, send_a_ref, send_b_ref, halo):
    even = lax.axis_index("space") % 2 == 0
    fill_halo(even, a_ref, b_ref, halo)
    apply_outer(outer_ref, part_ref, halo, y_ref)
    set_sends(even, y_ref, send_a_ref, send_b_ref)


def next_outer(part, a, b, outer):
    return pl.pallas_call(
        next_kernel,
        out_shape=(FIELD, HALO, HALO),
        in_specs=[VM] * 4,
        out_specs=(VM,) * 3,
        scratch_shapes=[pltpu.VMEM((2, 8, 256), jnp.float32)],
        compiler_params=params(6),
    )(part, a, b, outer)


def two_sum(a, b):
    s = a + b
    t = s - a
    return s, (a - (s - t)) + (b - t)


def halves(a):
    c = a * 4097.0
    high = c - (c - a)
    return high, a - high


def two_product(a, b):
    p = a * b
    ah, al = halves(a)
    bh, bl = halves(b)
    return p, ((ah * bh - p) + ah * bl + al * bh) + al * bl


def pair_add(x, y):
    s, e = two_sum(x[0], y[0])
    e = e + (x[1] + y[1])
    high = s + e
    return high, e - (high - s)


def pair_times(x, y):
    p, e = two_product(x[0], y[0])
    return p, e + (x[0] * y[1] + x[1] * y[0])


def last_kernel(part_ref, a_ref, b_ref, outer_ref, p0_ref, p1_ref, p2_ref, y_ref, m_ref, halo):
    even = lax.axis_index("space") % 2 == 0
    fill_halo(even, a_ref, b_ref, halo)
    apply_outer(outer_ref, part_ref, halo, y_ref)
    powers = [p0_ref, p1_ref, p2_ref, y_ref]
    row = lax.broadcasted_iota(jnp.int32, (8, 128), 0)
    lane = lax.broadcasted_iota(jnp.int32, (8, 128), 1)
    sums = []
    for f in range(2):
        packed = [jnp.zeros((8, 128), jnp.float32)] * 2
        for k in range(2 * ITERS):
            p, e = two_product(powers[k // 2][f], powers[(k + 1) // 2][f])
            total = pair_add((p[:, :128], e[:, :128]), (p[:, 128:], e[:, 128:]))
            for shift in (4, 2, 1):
                total = pair_add(total, [pltpu.roll(x, shift, 0) for x in total])
            packed = [jnp.where(row == k, x, y) for x, y in zip(total, packed)]
        for shift in (64, 32, 16, 8, 4, 2, 1):
            packed = pair_add(packed, [pltpu.roll(x, shift, 1) for x in packed])
        sums.append(packed)
    high = jnp.where(lane < 32, sums[0][0], sums[1][0])
    low = jnp.where(lane < 96, sums[0][1], sums[1][1])
    out = jnp.where((lane & 7) == row, jnp.where(lane < 64, high, low), 0.0)
    for shift in (4, 2, 1):
        out = out + pltpu.roll(out, shift, 0)
    out = out[0:1]
    for k in range(32):
        m_ref[k] = out


def last_outer(part, a, b, outer, p0, p1, p2):
    return pl.pallas_call(
        last_kernel,
        out_shape=(FIELD, jax.ShapeDtypeStruct((32, 1, 128), jnp.float32)),
        in_specs=[VM] * 7,
        out_specs=(VM,) * 2,
        scratch_shapes=[pltpu.VMEM((2, 8, 256), jnp.float32)],
        compiler_params=params(6),
    )(part, a, b, outer, p0, p1, p2)


def square_dot(poly, moment):
    total = None
    for k in range(2 * len(poly) - 1):
        coefficient = None
        for i in range(len(poly)):
            j = k - i
            if i > j or j >= len(poly):
                continue
            term = two_product(poly[i], poly[j])
            if i != j:
                term = (2.0 * term[0], 2.0 * term[1])
            coefficient = term if coefficient is None else pair_add(coefficient, term)
        term = pair_times(coefficient, moment[k])
        total = term if total is None else pair_add(total, term)
    return total[0] + total[1]


def finish_kernel(m_ref, p0_ref, p1_ref, p2_ref, p3_ref, inc_ref, res_ref):
    member = lax.axis_index("member")
    sums = [(m_ref[k], jnp.zeros((1, 128), jnp.float32)) for k in range(32)]
    while len(sums) > 1:
        pairs = [(two_sum(x[0], y[0]), x[1] + y[1]) for x, y in zip(sums[::2], sums[1::2])]
        sums = [(p[0], p[1] + e) for p, e in pairs]
    s, e = sums[0]
    low = e + pltpu.roll(s, 64, 1)
    moment = [(s, low)]
    for k in range(1, 2 * ITERS):
        moment.append((pltpu.roll(s, 128 - k, 1), pltpu.roll(low, 128 - k, 1)))
    one = jnp.ones((1, 128), jnp.float32)
    residual, direction, increment = [one], [one], []
    norm_now = moment[0][0] + moment[0][1]
    for iteration in range(ITERS):
        step = norm_now / square_dot(direction, moment[1:])
        moved = [step * c for c in direction]
        increment = [x + y for x, y in zip(increment, moved)] + moved[len(increment) :]
        residual = residual[:1] + [
            (residual[i + 1] if i + 1 < len(residual) else 0.0) - c for i, c in enumerate(moved)
        ]
        if iteration + 1 < ITERS:
            norm_next = square_dot(residual, moment)
            ratio = norm_next / (norm_now + EPSILON)
            grown = [ratio * c for c in direction]
            direction = [x + y for x, y in zip(residual, grown)] + residual[len(grown) :]
            norm_now = norm_next
    shift = (128 - (member % 8) * 16) % 128
    upper = member >= 8
    powers = [p0_ref, p1_ref, p2_ref, p3_ref]
    for f in range(2):
        at = 32 * f
        mine = [
            pltpu.roll(jnp.where(upper, p[f, :, 128:], p[f, :, :128]), shift, 1) for p in powers
        ]
        inc = sum(c[:, at : at + 1] * x for c, x in zip(increment, mine)) * SCALE
        res = sum(c[:, at : at + 1] * x for c, x in zip(residual, mine))
        inc_ref[f] = inc[:, :16]
        res_ref[f] = res[:, :16]


def finish(m, p):
    shape = jax.ShapeDtypeStruct((2, 8, 16), jnp.float32)
    return pl.pallas_call(
        finish_kernel,
        out_shape=(shape, shape),
        in_specs=[VM] * 5,
        out_specs=(VM, VM),
        compiler_params=params(8),
    )(m, *p)


def on_device(anomalies, loc_blocks, tile_reach, obs_var, innovations):
    own = gather_members(pack(anomalies, tile_reach, obs_var, innovations))
    odd = lax.axis_index("space") % 2
    to_a = lax.dynamic_slice_in_dim(own, 128 * (1 - odd), PART, 1)
    to_b = lax.dynamic_slice_in_dim(own, 128 * odd, PART, 1)
    a, b = pair_swap(to_a, 0), pair_swap(to_b, 1)
    table, inner, p0, obs, part = inner_blocks(tile_reach, loc_blocks, own)
    outer, p1, to_a, to_b = outer_blocks(tile_reach, own, a, b, table, part)
    a, b = pair_swap(to_a, 0), pair_swap(to_b, 1)
    part = next_inner(p1, obs, inner)
    p2, to_a, to_b = next_outer(part, a, b, outer)
    a, b = pair_swap(to_a, 0), pair_swap(to_b, 1)
    part = next_inner(p2, obs, inner)
    p3, m = last_outer(part, a, b, outer, p0, p1, p2)
    m = lax.all_to_all(m, "space", 0, 0)
    return finish(m, [p0, p1, p2, p3])


def solution(mesh):
    in_specs = (
        P("member", "space", None),
        P(),
        P("space"),
        P("space", "member"),
        P(None, "space", "member"),
    )
    out_specs = (P(None, "space", "member"), P(None, "space", "member"))
    return jax.shard_map(
        on_device, mesh=mesh, in_specs=in_specs, out_specs=out_specs, check_vma=False
    )
```

```python
import jax
import jax.numpy as jnp
from jax import lax
from jax.experimental import pallas as pl
from jax.experimental.pallas import tpu as pltpu
from jax.sharding import PartitionSpec as P

W = 4
ITERS = 3
EPSILON = 1e-6
SCALE = 2.0**-8
MIB = 1 << 20
PACK_MIB = 63

VM = pl.BlockSpec(memory_space=pltpu.VMEM)
SM = pl.BlockSpec(memory_space=pltpu.SMEM)
HBM = pl.BlockSpec(memory_space=pltpu.HBM)

FIELDS = 128
PART = 144
CHUNK = 272

BASE = [0, 5, 9, 12, 14]
BASE_T = [0, 15, 19, 22, 24]
N_TABLE = 26

INNER = [(w, s) for w in range(8) for s in range(-W, W + 1) if 0 <= w + s < 8]
OUTER = [(w, s) for w in range(8) for s in range(-W, W + 1) if not 0 <= w + s < 8]


def params(mib):
    return pltpu.CompilerParams(vmem_limit_bytes=mib * MIB)


def pair_swap(block, offset):
    n, m = lax.axis_size("space"), lax.axis_size("member")
    route = []
    for i in range(n):
        j = i + 1 if (i + offset) % 2 == 0 else i - 1
        for k in range(m):
            route.append((i * m + k, (j % n) * m + (k if 0 <= j < n else k ^ 1)))
    return lax.ppermute(block, ("space", "member"), route)


def pack_kernel(
    anomalies_hbm, reach_hbm, obs_hbm, innovations_hbm, chunk_ref, x_ref, reach_ref, obs_ref, inn_ref, sems
):
    moves = [(anomalies_hbm, x_ref), (innovations_hbm, inn_ref), (obs_hbm, obs_ref), (reach_hbm, reach_ref)]
    copies = [pltpu.make_async_copy(x, y, sems.at[i]) for i, (x, y) in enumerate(moves)]
    for copy in copies:
        copy.start()
    for copy in copies:
        copy.wait()
    x = x_ref[...].astype(jnp.float32)
    rows = []
    for t in range(8):
        tile = x[:, t, :]
        rows += [tile[:, :128], tile[:, 128:]]
    lane = lax.broadcasted_iota(jnp.int32, (1, 128), 1)
    lines = []
    for a in range(3):
        block = inn_ref[a] if a < 2 else obs_ref[...]
        wide = jnp.concatenate([block, jnp.zeros((8, 112), jnp.float32)], axis=1)
        line = wide[0:1]
        for t in range(1, 8):
            line = line + pltpu.roll(wide[t : t + 1], 16 * t, 1)
        lines.append(line)
    values = jnp.concatenate(lines, axis=0)
    high = values.astype(jnp.bfloat16).astype(jnp.float32)
    rest = values - high
    middle = rest.astype(jnp.bfloat16).astype(jnp.float32)
    reach = jnp.zeros((1, 128), jnp.float32)
    for t in range(8):
        reach = reach + jnp.where(lane == t, reach_ref[t].astype(jnp.float32), 0.0)
    fields = jnp.concatenate(
        [high, middle, rest - middle, reach, jnp.zeros((6, 128), jnp.float32)], axis=0
    )
    chunk_ref[...] = jnp.concatenate(rows[:8] + [fields] + rows[8:], axis=0).astype(jnp.bfloat16)


def pack(anomalies, tile_reach, obs_var, innovations):
    return pl.pallas_call(
        pack_kernel,
        out_shape=jax.ShapeDtypeStruct((CHUNK, 128), jnp.bfloat16),
        in_specs=[HBM] * 4,
        out_specs=VM,
        scratch_shapes=[
            pltpu.VMEM(anomalies.shape, jnp.bfloat16),
            pltpu.SMEM((8,), jnp.int32),
            pltpu.VMEM(obs_var.shape, jnp.float32),
            pltpu.VMEM(innovations.shape, jnp.float32),
            pltpu.SemaphoreType.DMA((4,)),
        ],
        compiler_params=params(PACK_MIB),
    )(anomalies, tile_reach, obs_var, innovations)


def send_copies(source, target, half, sems):
    rows = pl.ds(pl.multiple_of(half * CHUNK, 16), CHUNK)
    moves = [pltpu.make_async_copy(source, target.at[k, rows], sems.at[k]) for k in range(8)]
    for move in moves:
        move.start()
    for move in moves:
        move.wait()


def own_half_kernel(chunk_ref, out_ref, sems):
    send_copies(chunk_ref, out_ref, lax.axis_index("member") % 2, sems)


def other_half_kernel(chunk_ref, same_ref, out_ref, sems):
    send_copies(chunk_ref, out_ref, 1 - lax.axis_index("member") % 2, sems)


def gather_members(chunk):
    m = lax.axis_size("member")
    other = lax.ppermute(chunk, "member", [(k, k ^ 1) for k in range(m)])
    shape = jax.ShapeDtypeStruct((8, 2 * CHUNK, 128), jnp.bfloat16)
    scratch = [pltpu.SemaphoreType.DMA((8,))]
    half = pl.pallas_call(
        own_half_kernel,
        out_shape=shape,
        in_specs=[HBM],
        out_specs=HBM,
        scratch_shapes=scratch,
        compiler_params=params(4),
        cost_estimate=pl.CostEstimate(flops=0, bytes_accessed=2 * MIB, transcendentals=0),
    )(chunk)
    both = pl.pallas_call(
        other_half_kernel,
        out_shape=shape,
        in_specs=[VM, HBM],
        out_specs=HBM,
        scratch_shapes=scratch,
        input_output_aliases={1: 0},
        compiler_params=params(4),
    )(other, half)
    groups = [[2 * z + y for z in range(8)] for y in range(2)]
    out = lax.all_to_all(both, "member", 0, 0, axis_index_groups=groups)
    return out.reshape(16, CHUNK, 128)


def swap_blocks(x):
    row = lax.broadcasted_iota(jnp.int32, (8, 128), 0)
    block = lax.broadcasted_iota(jnp.int32, (8, 128), 1) // 16
    for bit in (1, 2, 4):
        r, b = (row & bit) != 0, (block & bit) != 0
        up = pltpu.roll(pltpu.roll(x, 8 - bit, 0), 16 * bit, 1)
        down = pltpu.roll(pltpu.roll(x, bit, 0), 128 - 16 * bit, 1)
        x = jnp.where(r == b, x, jnp.where(b, up, down))
    return x


def unpack_fields(lines):
    lines = lines.astype(jnp.float32)
    out = []
    for a in range(3):
        value = lines[:, a] + (lines[:, 3 + a] + lines[:, 6 + a])
        out.append(jnp.concatenate([swap_blocks(value[:8]), swap_blocks(value[8:])], axis=1))
    return out


def row_products(a, b):
    return lax.dot_general(a, b, (((1,), (1,)), ((), ())), preferred_element_type=jnp.float32)


def tile_of(ref, row):
    return jnp.concatenate(
        [
            ref[:, pl.ds(row, 16), :].reshape(256, 128),
            ref[:, pl.ds(row + 16, 16), :].reshape(256, 128),
        ],
        axis=1,
    )


def table_entry(shift, reach_w, reach_o):
    d = abs(shift)
    if shift >= 0:
        last, base = jnp.minimum(reach_o, reach_w - d), BASE[d]
    else:
        last, base = jnp.minimum(reach_w, reach_o - d), BASE_T[d]
    return jnp.where(last >= 0, base + last, N_TABLE - 1)


def fill_table(loc_ref, t_ref):
    factor = SCALE / 255.0
    k = 0
    for d in range(W + 1):
        total = None
        for o in range(W + 1 - d):
            p = row_products(loc_ref[o + d], loc_ref[o])
            total = p if total is None else total + p
            t_ref[k] = total * factor
            k += 1
    for d in range(1, W + 1):
        total = None
        for o in range(W + 1 - d):
            p = row_products(loc_ref[o], loc_ref[o + d])
            total = p if total is None else total + p
            t_ref[k] = total * factor
            k += 1
    t_ref[k] = jnp.zeros(t_ref.shape[1:], jnp.float32)


FIELD = jax.ShapeDtypeStruct((2, 8, 256), jnp.float32)
HALO = jax.ShapeDtypeStruct((2, W, 256), jnp.float32)
ROWS = 64


def apply_blocks(pairs, block_ref, field_row):
    out = []
    for w in range(8):
        mine = [(k, w + shift) for k, (row, shift) in enumerate(pairs) if row == w]
        done = [[], []]
        for c in range(0, 256, ROWS):
            acc = [None, None]
            for k, other in mine:
                block = block_ref[k, c : c + ROWS, :]
                for f in range(2):
                    p = block * field_row(f, other)
                    p = p[:, :128] + p[:, 128:]
                    acc[f] = p if acc[f] is None else acc[f] + p
            for f in range(2):
                done[f].append(acc[f])
        for f in range(2):
            total = jnp.sum(jnp.concatenate(done[f], axis=0).T, axis=0, keepdims=True)
            out.append((f, w, total))
    return out


def apply_inner(inner_ref, p_ref, obs_ref, part_ref):
    for f, w, total in apply_blocks(INNER, inner_ref, lambda f, t: p_ref[f, t : t + 1, :]):
        own = (obs_ref[w : w + 1, :] * SCALE) * p_ref[f, w : w + 1, :]
        part_ref[f, w : w + 1, :] = total + own


def apply_outer(outer_ref, part_ref, halo, y_ref):
    def row(f, t):
        at = t + W if t < 0 else t - W
        return halo[f, at : at + 1, :]

    for f, w, total in apply_blocks(OUTER, outer_ref, row):
        y_ref[f, w : w + 1, :] = total + part_ref[f, w : w + 1, :]


def inner_kernel(
    reach_ref, loc_ref, own_ref, t_ref, h_ref, xt_ref, p0_ref, obs_ref, part_ref, xs
):
    fill_table(loc_ref, t_ref)
    for w in range(8):
        xs[w] = tile_of(own_ref, 32 * w + (16 if w >= 4 else 0))
    fields = unpack_fields(own_ref[:, FIELDS : FIELDS + 16, :])
    for f in range(2):
        p0_ref[f] = fields[f]
    obs_ref[...] = fields[2]
    for w in range(8):
        rows = xs[w].T
        xt_ref[w] = rows
        for shift in range(-W, W + 1):
            if (w, shift) not in INNER:
                continue
            entry = table_entry(shift, reach_ref[w], reach_ref[w + shift])
            covariance = jnp.dot(rows, xs[w + shift], preferred_element_type=jnp.float32)
            h_ref[INNER.index((w, shift))] = covariance * t_ref[entry]
    apply_inner(h_ref, p0_ref, obs_ref, part_ref)


def inner_blocks(reach, loc_blocks, own):
    return pl.pallas_call(
        inner_kernel,
        out_shape=(
            jax.ShapeDtypeStruct((N_TABLE, 256, 256), jnp.float32),
            jax.ShapeDtypeStruct((len(INNER), 256, 256), jnp.float32),
            jax.ShapeDtypeStruct((8, 256, 256), jnp.bfloat16),
            FIELD,
            jax.ShapeDtypeStruct((8, 256), jnp.float32),
            FIELD,
        ),
        in_specs=[SM, VM, VM],
        out_specs=(VM,) * 6,
        scratch_shapes=[pltpu.VMEM((8, 256, 256), jnp.bfloat16)],
        compiler_params=params(12),
        cost_estimate=pl.CostEstimate(
            flops=100 * 2 * 256**3, bytes_accessed=20 * MIB, transcendentals=0
        ),
    )(reach, loc_blocks, own)


def set_sends(even, p, a_ref, b_ref):
    for f in range(2):
        low, high = p[f, :W], p[f, W:]
        a_ref[f] = jnp.where(even, high, low)
        b_ref[f] = jnp.where(even, low, high)


def fill_halo(even, a, b, halo):
    for f in range(2):
        halo[f, :W] = jnp.where(even, b[f], a[f])
        halo[f, W:] = jnp.where(even, a[f], b[f])


def outer_kernel(
    reach_ref, xt_ref, a_ref, b_ref, t_ref, part_ref,
    outer_ref, y_ref, send_a_ref, send_b_ref,
    xs, lines, halo,
):
    even = lax.axis_index("space") % 2 == 0
    a_low, b_low = jnp.where(even, 0, 16), jnp.where(even, 16, 0)
    for w in range(W):
        xs[jnp.where(even, W, 0) + w] = tile_of(a_ref, pl.multiple_of(a_low + 32 * w, 16))
        xs[jnp.where(even, 0, W) + w] = tile_of(b_ref, pl.multiple_of(b_low + 32 * w, 16))
    a_at = pl.multiple_of(jnp.where(even, 128, 0), 16)
    b_at = pl.multiple_of(jnp.where(even, 0, 128), 16)
    lines[0] = a_ref[:, pl.ds(a_at, 16), :]
    lines[1] = b_ref[:, pl.ds(b_at, 16), :]

    lane = lax.broadcasted_iota(jnp.int32, (1, 128), 1)
    reach_a = lines[0, 0, 9:10, :].astype(jnp.float32)
    reach_b = lines[1, 0, 9:10, :].astype(jnp.float32)
    reach_left = jnp.where(even, reach_b, reach_a)
    reach_right = jnp.where(even, reach_a, reach_b)

    def reach_of(tile):
        if 0 <= tile < 8:
            return reach_ref[tile]
        line, at = (reach_left, tile + 8) if tile < 0 else (reach_right, tile - 8)
        return jnp.sum(jnp.where(lane == at, line, 0.0)).astype(jnp.int32)

    reach = {tile: reach_of(tile) for tile in range(-W, 8 + W)}
    a_fields, b_fields = unpack_fields(lines[0]), unpack_fields(lines[1])
    fill_halo(
        even,
        [jnp.where(even, x[:W], x[W:]) for x in a_fields[:2]],
        [jnp.where(even, x[W:], x[:W]) for x in b_fields[:2]],
        halo,
    )
    for w in range(8):
        rows = xt_ref[w]
        for shift in range(-W, W + 1):
            if (w, shift) not in OUTER:
                continue
            other = w + shift
            entry = table_entry(shift, reach[w], reach[other])
            tile = xs[other + W if other < 0 else other - W]
            covariance = jnp.dot(rows, tile, preferred_element_type=jnp.float32)
            outer_ref[OUTER.index((w, shift))] = covariance * t_ref[entry]
    apply_outer(outer_ref, part_ref, halo, y_ref)
    set_sends(even, y_ref, send_a_ref, send_b_ref)


def outer_blocks(reach, xt, a, b, table, part):
    return pl.pallas_call(
        outer_kernel,
        out_shape=(
            jax.ShapeDtypeStruct((len(OUTER), 256, 256), jnp.float32),
            FIELD,
            HALO,
            HALO,
        ),
        in_specs=[SM] + [VM] * 5,
        out_specs=(VM,) * 4,
        scratch_shapes=[
            pltpu.VMEM((8, 256, 256), jnp.bfloat16),
            pltpu.VMEM((2, 16, 16, 128), jnp.bfloat16),
            pltpu.VMEM((2, 8, 256), jnp.float32),
        ],
        compiler_params=params(12),
    )(reach, xt, a, b, table, part)


def next_inner(p, obs, inner):
    return pl.pallas_call(
        lambda p_ref, obs_ref, inner_ref, part_ref: apply_inner(inner_ref, p_ref, obs_ref, part_ref),
        out_shape=FIELD,
        in_specs=[VM] * 3,
        out_specs=VM,
        compiler_params=params(6),
        cost_estimate=pl.CostEstimate(
            flops=50 * 2 * 256**3, bytes_accessed=14 * MIB, transcendentals=0
        ),
    )(p, obs, inner)


def next_kernel(part_ref, a_ref, b_ref, outer_ref, y_ref, send_a_ref, send_b_ref, halo):
    even = lax.axis_index("space") % 2 == 0
    fill_halo(even, a_ref, b_ref, halo)
    apply_outer(outer_ref, part_ref, halo, y_ref)
    set_sends(even, y_ref, send_a_ref, send_b_ref)


def next_outer(part, a, b, outer):
    return pl.pallas_call(
        next_kernel,
        out_shape=(FIELD, HALO, HALO),
        in_specs=[VM] * 4,
        out_specs=(VM,) * 3,
        scratch_shapes=[pltpu.VMEM((2, 8, 256), jnp.float32)],
        compiler_params=params(6),
    )(part, a, b, outer)


def two_sum(a, b):
    s = a + b
    t = s - a
    return s, (a - (s - t)) + (b - t)


def halves(a):
    c = a * 4097.0
    high = c - (c - a)
    return high, a - high


def two_product(a, b):
    p = a * b
    ah, al = halves(a)
    bh, bl = halves(b)
    return p, ((ah * bh - p) + ah * bl + al * bh) + al * bl


def pair_add(x, y):
    s, e = two_sum(x[0], y[0])
    e = e + (x[1] + y[1])
    high = s + e
    return high, e - (high - s)


def pair_times(x, y):
    p, e = two_product(x[0], y[0])
    return p, e + (x[0] * y[1] + x[1] * y[0])


def last_kernel(part_ref, a_ref, b_ref, outer_ref, p0_ref, p1_ref, p2_ref, y_ref, m_ref, halo):
    even = lax.axis_index("space") % 2 == 0
    fill_halo(even, a_ref, b_ref, halo)
    apply_outer(outer_ref, part_ref, halo, y_ref)
    powers = [p0_ref, p1_ref, p2_ref, y_ref]
    row = lax.broadcasted_iota(jnp.int32, (8, 128), 0)
    lane = lax.broadcasted_iota(jnp.int32, (8, 128), 1)
    sums = []
    for f in range(2):
        packed = [jnp.zeros((8, 128), jnp.float32)] * 2
        for k in range(2 * ITERS):
            p, e = two_product(powers[k // 2][f], powers[(k + 1) // 2][f])
            total = pair_add((p[:, :128], e[:, :128]), (p[:, 128:], e[:, 128:]))
            for shift in (4, 2, 1):
                total = pair_add(total, [pltpu.roll(x, shift, 0) for x in total])
            packed = [jnp.where(row == k, x, y) for x, y in zip(total, packed)]
        for shift in (64, 32, 16, 8, 4, 2, 1):
            packed = pair_add(packed, [pltpu.roll(x, shift, 1) for x in packed])
        sums.append(packed)
    high = jnp.where(lane < 32, sums[0][0], sums[1][0])
    low = jnp.where(lane < 96, sums[0][1], sums[1][1])
    out = jnp.where((lane & 7) == row, jnp.where(lane < 64, high, low), 0.0)
    for shift in (4, 2, 1):
        out = out + pltpu.roll(out, shift, 0)
    out = out[0:1]
    for k in range(32):
        m_ref[k] = out


def last_outer(part, a, b, outer, p0, p1, p2):
    return pl.pallas_call(
        last_kernel,
        out_shape=(FIELD, jax.ShapeDtypeStruct((32, 1, 128), jnp.float32)),
        in_specs=[VM] * 7,
        out_specs=(VM,) * 2,
        scratch_shapes=[pltpu.VMEM((2, 8, 256), jnp.float32)],
        compiler_params=params(6),
    )(part, a, b, outer, p0, p1, p2)


def square_dot(poly, moment):
    total = None
    for k in range(2 * len(poly) - 1):
        coefficient = None
        for i in range(len(poly)):
            j = k - i
            if i > j or j >= len(poly):
                continue
            term = two_product(poly[i], poly[j])
            if i != j:
                term = (2.0 * term[0], 2.0 * term[1])
            coefficient = term if coefficient is None else pair_add(coefficient, term)
        term = pair_times(coefficient, moment[k])
        total = term if total is None else pair_add(total, term)
    return total[0] + total[1]


def finish_kernel(m_ref, p0_ref, p1_ref, p2_ref, p3_ref, inc_ref, res_ref):
    member = lax.axis_index("member")
    sums = [(m_ref[k], jnp.zeros((1, 128), jnp.float32)) for k in range(32)]
    while len(sums) > 1:
        pairs = [(two_sum(x[0], y[0]), x[1] + y[1]) for x, y in zip(sums[::2], sums[1::2])]
        sums = [(p[0], p[1] + e) for p, e in pairs]
    s, e = sums[0]
    low = e + pltpu.roll(s, 64, 1)
    moment = [(s, low)]
    for k in range(1, 2 * ITERS):
        moment.append((pltpu.roll(s, 128 - k, 1), pltpu.roll(low, 128 - k, 1)))
    one = jnp.ones((1, 128), jnp.float32)
    residual, direction, increment = [one], [one], []
    norm_now = moment[0][0] + moment[0][1]
    for iteration in range(ITERS):
        step = norm_now / square_dot(direction, moment[1:])
        moved = [step * c for c in direction]
        increment = [x + y for x, y in zip(increment, moved)] + moved[len(increment) :]
        residual = residual[:1] + [
            (residual[i + 1] if i + 1 < len(residual) else 0.0) - c for i, c in enumerate(moved)
        ]
        if iteration + 1 < ITERS:
            norm_next = square_dot(residual, moment)
            ratio = norm_next / (norm_now + EPSILON)
            grown = [ratio * c for c in direction]
            direction = [x + y for x, y in zip(residual, grown)] + residual[len(grown) :]
            norm_now = norm_next
    shift = (128 - (member % 8) * 16) % 128
    upper = member >= 8
    powers = [p0_ref, p1_ref, p2_ref, p3_ref]
    for f in range(2):
        at = 32 * f
        mine = [
            pltpu.roll(jnp.where(upper, p[f, :, 128:], p[f, :, :128]), shift, 1) for p in powers
        ]
        inc = sum(c[:, at : at + 1] * x for c, x in zip(increment, mine)) * SCALE
        res = sum(c[:, at : at + 1] * x for c, x in zip(residual, mine))
        inc_ref[f] = inc[:, :16]
        res_ref[f] = res[:, :16]


def finish(m, p):
    shape = jax.ShapeDtypeStruct((2, 8, 16), jnp.float32)
    return pl.pallas_call(
        finish_kernel,
        out_shape=(shape, shape),
        in_specs=[VM] * 5,
        out_specs=(VM, VM),
        compiler_params=params(8),
    )(m, *p)


def on_device(anomalies, loc_blocks, tile_reach, obs_var, innovations):
    own = gather_members(pack(anomalies, tile_reach, obs_var, innovations))
    own, loc_blocks, tile_reach = lax.optimization_barrier((own, loc_blocks, tile_reach))
    odd = lax.axis_index("space") % 2
    to_a = lax.dynamic_slice_in_dim(own, 128 * (1 - odd), PART, 1)
    to_b = lax.dynamic_slice_in_dim(own, 128 * odd, PART, 1)
    b = pair_swap(to_b, 1)
    a = pair_swap(to_a, 0)
    table, inner, xt, p0, obs, part = inner_blocks(tile_reach, loc_blocks, own)
    outer, p1, to_a, to_b = outer_blocks(tile_reach, xt, a, b, table, part)
    a, b = pair_swap(to_a, 0), pair_swap(to_b, 1)
    part = next_inner(p1, obs, inner)
    p2, to_a, to_b = next_outer(part, a, b, outer)
    a, b = pair_swap(to_a, 0), pair_swap(to_b, 1)
    part = next_inner(p2, obs, inner)
    p3, m = last_outer(part, a, b, outer, p0, p1, p2)
    m = lax.all_to_all(m, "space", 0, 0)
    return finish(m, [p0, p1, p2, p3])


def solution(mesh):
    in_specs = (
        P("member", "space", None),
        P(),
        P("space"),
        P("space", "member"),
        P(None, "space", "member"),
    )
    out_specs = (P(None, "space", "member"), P(None, "space", "member"))
    return jax.shard_map(
        on_device, mesh=mesh, in_specs=in_specs, out_specs=out_specs, check_vma=False
    )
```

```python
import jax
import jax.numpy as jnp
from jax import lax
from jax.experimental import pallas as pl
from jax.experimental.pallas import tpu as pltpu
from jax.sharding import PartitionSpec as P

W = 4
ITERS = 3
EPSILON = 1e-6
SCALE = 2.0**-8
MIB = 1 << 20
PACK_MIB = 63

VM = pl.BlockSpec(memory_space=pltpu.VMEM)
SM = pl.BlockSpec(memory_space=pltpu.SMEM)
HBM = pl.BlockSpec(memory_space=pltpu.HBM)

FIELDS = 128
PART = 144
CHUNK = 272

BASE = [0, 5, 9, 12, 14]
BASE_T = [0, 15, 19, 22, 24]
N_TABLE = 26

INNER = [(w, s) for w in range(8) for s in range(-W, W + 1) if 0 <= w + s < 8]
OUTER = [(w, s) for w in range(8) for s in range(-W, W + 1) if not 0 <= w + s < 8]


def params(mib):
    return pltpu.CompilerParams(vmem_limit_bytes=mib * MIB)


def pair_swap(block, offset):
    n, m = lax.axis_size("space"), lax.axis_size("member")
    route = []
    for i in range(n):
        j = i + 1 if (i + offset) % 2 == 0 else i - 1
        for k in range(m):
            route.append((i * m + k, (j % n) * m + (k if 0 <= j < n else k ^ 1)))
    return lax.ppermute(block, ("space", "member"), route)


def pack_kernel(
    anomalies_hbm, reach_hbm, obs_hbm, innovations_hbm, chunk_ref, x_ref, reach_ref, obs_ref, inn_ref, sems
):
    moves = [(anomalies_hbm, x_ref), (innovations_hbm, inn_ref), (obs_hbm, obs_ref), (reach_hbm, reach_ref)]
    copies = [pltpu.make_async_copy(x, y, sems.at[i]) for i, (x, y) in enumerate(moves)]
    for copy in copies:
        copy.start()
    for copy in copies:
        copy.wait()
    x = x_ref[...].astype(jnp.float32)
    rows = []
    for t in range(8):
        tile = x[:, t, :]
        rows += [tile[:, :128], tile[:, 128:]]
    lane = lax.broadcasted_iota(jnp.int32, (1, 128), 1)
    lines = []
    for a in range(3):
        block = inn_ref[a] if a < 2 else obs_ref[...]
        wide = jnp.concatenate([block, jnp.zeros((8, 112), jnp.float32)], axis=1)
        line = wide[0:1]
        for t in range(1, 8):
            line = line + pltpu.roll(wide[t : t + 1], 16 * t, 1)
        lines.append(line)
    values = jnp.concatenate(lines, axis=0)
    high = values.astype(jnp.bfloat16).astype(jnp.float32)
    rest = values - high
    middle = rest.astype(jnp.bfloat16).astype(jnp.float32)
    reach = jnp.zeros((1, 128), jnp.float32)
    for t in range(8):
        reach = reach + jnp.where(lane == t, reach_ref[t].astype(jnp.float32), 0.0)
    fields = jnp.concatenate(
        [high, middle, rest - middle, reach, jnp.zeros((6, 128), jnp.float32)], axis=0
    )
    chunk_ref[...] = jnp.concatenate(rows[:8] + [fields] + rows[8:], axis=0).astype(jnp.bfloat16)


def pack(anomalies, tile_reach, obs_var, innovations):
    return pl.pallas_call(
        pack_kernel,
        out_shape=jax.ShapeDtypeStruct((CHUNK, 128), jnp.bfloat16),
        in_specs=[HBM] * 4,
        out_specs=VM,
        scratch_shapes=[
            pltpu.VMEM(anomalies.shape, jnp.bfloat16),
            pltpu.SMEM((8,), jnp.int32),
            pltpu.VMEM(obs_var.shape, jnp.float32),
            pltpu.VMEM(innovations.shape, jnp.float32),
            pltpu.SemaphoreType.DMA((4,)),
        ],
        compiler_params=params(PACK_MIB),
    )(anomalies, tile_reach, obs_var, innovations)


def send_copies(source, target, half, sems):
    rows = pl.ds(pl.multiple_of(half * CHUNK, 16), CHUNK)
    moves = [pltpu.make_async_copy(source, target.at[k, rows], sems.at[k]) for k in range(8)]
    for move in moves:
        move.start()
    for move in moves:
        move.wait()


def own_half_kernel(chunk_ref, out_ref, sems):
    send_copies(chunk_ref, out_ref, lax.axis_index("member") % 2, sems)


def other_half_kernel(chunk_ref, same_ref, out_ref, sems):
    send_copies(chunk_ref, out_ref, 1 - lax.axis_index("member") % 2, sems)


def gather_members(chunk):
    m = lax.axis_size("member")
    other = lax.ppermute(chunk, "member", [(k, k ^ 1) for k in range(m)])
    shape = jax.ShapeDtypeStruct((8, 2 * CHUNK, 128), jnp.bfloat16)
    scratch = [pltpu.SemaphoreType.DMA((8,))]
    half = pl.pallas_call(
        own_half_kernel,
        out_shape=shape,
        in_specs=[HBM],
        out_specs=HBM,
        scratch_shapes=scratch,
        compiler_params=params(4),
        cost_estimate=pl.CostEstimate(flops=0, bytes_accessed=2 * MIB, transcendentals=0),
    )(chunk)
    both = pl.pallas_call(
        other_half_kernel,
        out_shape=shape,
        in_specs=[VM, HBM],
        out_specs=HBM,
        scratch_shapes=scratch,
        input_output_aliases={1: 0},
        compiler_params=params(4),
    )(other, half)
    groups = [[2 * z + y for z in range(8)] for y in range(2)]
    out = lax.all_to_all(both, "member", 0, 0, axis_index_groups=groups)
    return out.reshape(16, CHUNK, 128)


def swap_blocks(x):
    row = lax.broadcasted_iota(jnp.int32, (8, 128), 0)
    block = lax.broadcasted_iota(jnp.int32, (8, 128), 1) // 16
    for bit in (1, 2, 4):
        r, b = (row & bit) != 0, (block & bit) != 0
        up = pltpu.roll(pltpu.roll(x, 8 - bit, 0), 16 * bit, 1)
        down = pltpu.roll(pltpu.roll(x, bit, 0), 128 - 16 * bit, 1)
        x = jnp.where(r == b, x, jnp.where(b, up, down))
    return x


def unpack_fields(lines):
    lines = lines.astype(jnp.float32)
    out = []
    for a in range(3):
        value = lines[:, a] + (lines[:, 3 + a] + lines[:, 6 + a])
        out.append(jnp.concatenate([swap_blocks(value[:8]), swap_blocks(value[8:])], axis=1))
    return out


def row_products(a, b):
    return lax.dot_general(a, b, (((1,), (1,)), ((), ())), preferred_element_type=jnp.float32)


def tile_of(ref, row):
    return jnp.concatenate(
        [
            ref[:, pl.ds(row, 16), :].reshape(256, 128),
            ref[:, pl.ds(row + 16, 16), :].reshape(256, 128),
        ],
        axis=1,
    )


def table_entry(shift, reach_w, reach_o):
    d = abs(shift)
    if shift >= 0:
        last, base = jnp.minimum(reach_o, reach_w - d), BASE[d]
    else:
        last, base = jnp.minimum(reach_w, reach_o - d), BASE_T[d]
    return jnp.where(last >= 0, base + last, N_TABLE - 1)


def fill_table(loc_ref, t_ref):
    factor = SCALE / 255.0
    k = 0
    for d in range(W + 1):
        total = None
        for o in range(W + 1 - d):
            p = row_products(loc_ref[o + d], loc_ref[o])
            total = p if total is None else total + p
            t_ref[k] = total * factor
            k += 1
    for d in range(1, W + 1):
        total = None
        for o in range(W + 1 - d):
            p = row_products(loc_ref[o], loc_ref[o + d])
            total = p if total is None else total + p
            t_ref[k] = total * factor
            k += 1
    t_ref[k] = jnp.zeros(t_ref.shape[1:], jnp.float32)


FIELD = jax.ShapeDtypeStruct((2, 8, 256), jnp.float32)
HALO = jax.ShapeDtypeStruct((2, W, 256), jnp.float32)
ROWS = 64


def apply_blocks(pairs, block_ref, field_row):
    out = []
    for w in range(8):
        mine = [(k, w + shift) for k, (row, shift) in enumerate(pairs) if row == w]
        done = [[], []]
        for c in range(0, 256, ROWS):
            acc = [None, None]
            for k, other in mine:
                block = block_ref[k, c : c + ROWS, :]
                for f in range(2):
                    p = block * field_row(f, other)
                    p = p[:, :128] + p[:, 128:]
                    acc[f] = p if acc[f] is None else acc[f] + p
            for f in range(2):
                done[f].append(acc[f])
        for f in range(2):
            total = jnp.sum(jnp.concatenate(done[f], axis=0).T, axis=0, keepdims=True)
            out.append((f, w, total))
    return out


def apply_inner(inner_ref, p_ref, obs_ref, part_ref):
    for f, w, total in apply_blocks(INNER, inner_ref, lambda f, t: p_ref[f, t : t + 1, :]):
        own = (obs_ref[w : w + 1, :] * SCALE) * p_ref[f, w : w + 1, :]
        part_ref[f, w : w + 1, :] = total + own


def apply_outer(outer_ref, part_ref, halo, y_ref):
    def row(f, t):
        at = t + W if t < 0 else t - W
        return halo[f, at : at + 1, :]

    for f, w, total in apply_blocks(OUTER, outer_ref, row):
        y_ref[f, w : w + 1, :] = total + part_ref[f, w : w + 1, :]


def inner_kernel(
    reach_ref, loc_ref, own_ref, t_ref, h_ref, xt_ref, p0_ref, obs_ref, part_ref, xs
):
    fill_table(loc_ref, t_ref)
    for w in range(8):
        xs[w] = tile_of(own_ref, 32 * w + (16 if w >= 4 else 0))
    fields = unpack_fields(own_ref[:, FIELDS : FIELDS + 16, :])
    for f in range(2):
        p0_ref[f] = fields[f]
    obs_ref[...] = fields[2]
    for w in range(8):
        rows = xs[w].T
        xt_ref[w] = rows
        for shift in range(-W, W + 1):
            if (w, shift) not in INNER:
                continue
            entry = table_entry(shift, reach_ref[w], reach_ref[w + shift])
            covariance = jnp.dot(rows, xs[w + shift], preferred_element_type=jnp.float32)
            h_ref[INNER.index((w, shift))] = covariance * t_ref[entry]
    apply_inner(h_ref, p0_ref, obs_ref, part_ref)


def inner_blocks(reach, loc_blocks, own):
    return pl.pallas_call(
        inner_kernel,
        out_shape=(
            jax.ShapeDtypeStruct((N_TABLE, 256, 256), jnp.float32),
            jax.ShapeDtypeStruct((len(INNER), 256, 256), jnp.float32),
            jax.ShapeDtypeStruct((8, 256, 256), jnp.bfloat16),
            FIELD,
            jax.ShapeDtypeStruct((8, 256), jnp.float32),
            FIELD,
        ),
        in_specs=[SM, VM, VM],
        out_specs=(VM,) * 6,
        scratch_shapes=[pltpu.VMEM((8, 256, 256), jnp.bfloat16)],
        compiler_params=params(12),
        cost_estimate=pl.CostEstimate(
            flops=100 * 2 * 256**3, bytes_accessed=20 * MIB, transcendentals=0
        ),
    )(reach, loc_blocks, own)


def set_sends(even, p, a_ref, b_ref):
    for f in range(2):
        low, high = p[f, :W], p[f, W:]
        a_ref[f] = jnp.where(even, high, low)
        b_ref[f] = jnp.where(even, low, high)


def fill_halo(even, a, b, halo):
    for f in range(2):
        halo[f, :W] = jnp.where(even, b[f], a[f])
        halo[f, W:] = jnp.where(even, a[f], b[f])


def outer_kernel(
    reach_ref, xt_ref, a_ref, b_ref, t_ref, part_ref,
    outer_ref, y_ref, send_a_ref, send_b_ref,
    xs, lines, halo,
):
    even = lax.axis_index("space") % 2 == 0
    a_low, b_low = jnp.where(even, 0, 16), jnp.where(even, 16, 0)
    for w in range(W):
        xs[jnp.where(even, W, 0) + w] = tile_of(a_ref, pl.multiple_of(a_low + 32 * w, 16))
        xs[jnp.where(even, 0, W) + w] = tile_of(b_ref, pl.multiple_of(b_low + 32 * w, 16))
    a_at = pl.multiple_of(jnp.where(even, 128, 0), 16)
    b_at = pl.multiple_of(jnp.where(even, 0, 128), 16)
    lines[0] = a_ref[:, pl.ds(a_at, 16), :]
    lines[1] = b_ref[:, pl.ds(b_at, 16), :]

    lane = lax.broadcasted_iota(jnp.int32, (1, 128), 1)
    reach_a = lines[0, 0, 9:10, :].astype(jnp.float32)
    reach_b = lines[1, 0, 9:10, :].astype(jnp.float32)
    reach_left = jnp.where(even, reach_b, reach_a)
    reach_right = jnp.where(even, reach_a, reach_b)

    def reach_of(tile):
        if 0 <= tile < 8:
            return reach_ref[tile]
        line, at = (reach_left, tile + 8) if tile < 0 else (reach_right, tile - 8)
        return jnp.sum(jnp.where(lane == at, line, 0.0)).astype(jnp.int32)

    reach = {tile: reach_of(tile) for tile in range(-W, 8 + W)}
    a_fields, b_fields = unpack_fields(lines[0]), unpack_fields(lines[1])
    fill_halo(
        even,
        [jnp.where(even, x[:W], x[W:]) for x in a_fields[:2]],
        [jnp.where(even, x[W:], x[:W]) for x in b_fields[:2]],
        halo,
    )
    for w in range(8):
        rows = xt_ref[w]
        for shift in range(-W, W + 1):
            if (w, shift) not in OUTER:
                continue
            other = w + shift
            entry = table_entry(shift, reach[w], reach[other])
            tile = xs[other + W if other < 0 else other - W]
            covariance = jnp.dot(rows, tile, preferred_element_type=jnp.float32)
            outer_ref[OUTER.index((w, shift))] = covariance * t_ref[entry]
    apply_outer(outer_ref, part_ref, halo, y_ref)
    set_sends(even, y_ref, send_a_ref, send_b_ref)


def outer_blocks(reach, xt, a, b, table, part):
    return pl.pallas_call(
        outer_kernel,
        out_shape=(
            jax.ShapeDtypeStruct((len(OUTER), 256, 256), jnp.float32),
            FIELD,
            HALO,
            HALO,
        ),
        in_specs=[SM] + [VM] * 5,
        out_specs=(VM,) * 4,
        scratch_shapes=[
            pltpu.VMEM((8, 256, 256), jnp.bfloat16),
            pltpu.VMEM((2, 16, 16, 128), jnp.bfloat16),
            pltpu.VMEM((2, 8, 256), jnp.float32),
        ],
        compiler_params=params(12),
    )(reach, xt, a, b, table, part)


def next_inner(p, obs, inner):
    return pl.pallas_call(
        lambda p_ref, obs_ref, inner_ref, part_ref: apply_inner(inner_ref, p_ref, obs_ref, part_ref),
        out_shape=FIELD,
        in_specs=[VM] * 3,
        out_specs=VM,
        compiler_params=params(6),
        cost_estimate=pl.CostEstimate(
            flops=50 * 2 * 256**3, bytes_accessed=14 * MIB, transcendentals=0
        ),
    )(p, obs, inner)


def next_kernel(part_ref, b_ref, a_ref, outer_ref, y_ref, send_a_ref, send_b_ref, halo):
    even = lax.axis_index("space") % 2 == 0
    fill_halo(even, a_ref, b_ref, halo)
    apply_outer(outer_ref, part_ref, halo, y_ref)
    set_sends(even, y_ref, send_a_ref, send_b_ref)


def next_outer(part, a, b, outer):
    return pl.pallas_call(
        next_kernel,
        out_shape=(FIELD, HALO, HALO),
        in_specs=[VM] * 4,
        out_specs=(VM,) * 3,
        scratch_shapes=[pltpu.VMEM((2, 8, 256), jnp.float32)],
        compiler_params=params(6),
    )(part, b, a, outer)


def two_sum(a, b):
    s = a + b
    t = s - a
    return s, (a - (s - t)) + (b - t)


def halves(a):
    c = a * 4097.0
    high = c - (c - a)
    return high, a - high


def two_product(a, b):
    p = a * b
    ah, al = halves(a)
    bh, bl = halves(b)
    return p, ((ah * bh - p) + ah * bl + al * bh) + al * bl


def pair_add(x, y):
    s, e = two_sum(x[0], y[0])
    e = e + (x[1] + y[1])
    high = s + e
    return high, e - (high - s)


def pair_times(x, y):
    p, e = two_product(x[0], y[0])
    return p, e + (x[0] * y[1] + x[1] * y[0])


def last_kernel(part_ref, b_ref, a_ref, outer_ref, p0_ref, p1_ref, p2_ref, y_ref, m_ref, halo):
    even = lax.axis_index("space") % 2 == 0
    fill_halo(even, a_ref, b_ref, halo)
    apply_outer(outer_ref, part_ref, halo, y_ref)
    powers = [p0_ref, p1_ref, p2_ref, y_ref]
    row = lax.broadcasted_iota(jnp.int32, (8, 128), 0)
    lane = lax.broadcasted_iota(jnp.int32, (8, 128), 1)
    sums = []
    for f in range(2):
        packed = [jnp.zeros((8, 128), jnp.float32)] * 2
        for k in range(2 * ITERS):
            p, e = two_product(powers[k // 2][f], powers[(k + 1) // 2][f])
            total = pair_add((p[:, :128], e[:, :128]), (p[:, 128:], e[:, 128:]))
            for shift in (4, 2, 1):
                total = pair_add(total, [pltpu.roll(x, shift, 0) for x in total])
            packed = [jnp.where(row == k, x, y) for x, y in zip(total, packed)]
        for shift in (64, 32, 16, 8, 4, 2, 1):
            packed = pair_add(packed, [pltpu.roll(x, shift, 1) for x in packed])
        sums.append(packed)
    high = jnp.where(lane < 32, sums[0][0], sums[1][0])
    low = jnp.where(lane < 96, sums[0][1], sums[1][1])
    out = jnp.where((lane & 7) == row, jnp.where(lane < 64, high, low), 0.0)
    for shift in (4, 2, 1):
        out = out + pltpu.roll(out, shift, 0)
    out = out[0:1]
    for k in range(32):
        m_ref[k] = out


def last_outer(part, a, b, outer, p0, p1, p2):
    return pl.pallas_call(
        last_kernel,
        out_shape=(FIELD, jax.ShapeDtypeStruct((32, 1, 128), jnp.float32)),
        in_specs=[VM] * 7,
        out_specs=(VM,) * 2,
        scratch_shapes=[pltpu.VMEM((2, 8, 256), jnp.float32)],
        compiler_params=params(6),
    )(part, b, a, outer, p0, p1, p2)


def square_dot(poly, moment):
    total = None
    for k in range(2 * len(poly) - 1):
        coefficient = None
        for i in range(len(poly)):
            j = k - i
            if i > j or j >= len(poly):
                continue
            term = two_product(poly[i], poly[j])
            if i != j:
                term = (2.0 * term[0], 2.0 * term[1])
            coefficient = term if coefficient is None else pair_add(coefficient, term)
        term = pair_times(coefficient, moment[k])
        total = term if total is None else pair_add(total, term)
    return total[0] + total[1]


def finish_kernel(m_ref, p0_ref, p1_ref, p2_ref, p3_ref, inc_ref, res_ref):
    member = lax.axis_index("member")
    sums = [(m_ref[k], jnp.zeros((1, 128), jnp.float32)) for k in range(32)]
    while len(sums) > 1:
        pairs = [(two_sum(x[0], y[0]), x[1] + y[1]) for x, y in zip(sums[::2], sums[1::2])]
        sums = [(p[0], p[1] + e) for p, e in pairs]
    s, e = sums[0]
    low = e + pltpu.roll(s, 64, 1)
    moment = [(s, low)]
    for k in range(1, 2 * ITERS):
        moment.append((pltpu.roll(s, 128 - k, 1), pltpu.roll(low, 128 - k, 1)))
    one = jnp.ones((1, 128), jnp.float32)
    residual, direction, increment = [one], [one], []
    norm_now = moment[0][0] + moment[0][1]
    for iteration in range(ITERS):
        step = norm_now / square_dot(direction, moment[1:])
        moved = [step * c for c in direction]
        increment = [x + y for x, y in zip(increment, moved)] + moved[len(increment) :]
        residual = residual[:1] + [
            (residual[i + 1] if i + 1 < len(residual) else 0.0) - c for i, c in enumerate(moved)
        ]
        if iteration + 1 < ITERS:
            norm_next = square_dot(residual, moment)
            ratio = norm_next / (norm_now + EPSILON)
            grown = [ratio * c for c in direction]
            direction = [x + y for x, y in zip(residual, grown)] + residual[len(grown) :]
            norm_now = norm_next
    shift = (128 - (member % 8) * 16) % 128
    upper = member >= 8
    powers = [p0_ref, p1_ref, p2_ref, p3_ref]
    for f in range(2):
        at = 32 * f
        mine = [
            pltpu.roll(jnp.where(upper, p[f, :, 128:], p[f, :, :128]), shift, 1) for p in powers
        ]
        inc = sum(c[:, at : at + 1] * x for c, x in zip(increment, mine)) * SCALE
        res = sum(c[:, at : at + 1] * x for c, x in zip(residual, mine))
        inc_ref[f] = inc[:, :16]
        res_ref[f] = res[:, :16]


def finish(m, p):
    shape = jax.ShapeDtypeStruct((2, 8, 16), jnp.float32)
    return pl.pallas_call(
        finish_kernel,
        out_shape=(shape, shape),
        in_specs=[VM] * 5,
        out_specs=(VM, VM),
        compiler_params=params(8),
    )(m, *p)


def on_device(anomalies, loc_blocks, tile_reach, obs_var, innovations):
    own = gather_members(pack(anomalies, tile_reach, obs_var, innovations))
    own, loc_blocks, tile_reach = lax.optimization_barrier((own, loc_blocks, tile_reach))
    odd = lax.axis_index("space") % 2
    to_a = lax.dynamic_slice_in_dim(own, 128 * (1 - odd), PART, 1)
    to_b = lax.dynamic_slice_in_dim(own, 128 * odd, PART, 1)
    b = pair_swap(to_b, 1)
    a = pair_swap(to_a, 0)
    table, inner, xt, p0, obs, part = inner_blocks(tile_reach, loc_blocks, own)
    outer, p1, to_a, to_b = outer_blocks(tile_reach, xt, a, b, table, part)
    a, b = pair_swap(to_a, 0), pair_swap(to_b, 1)
    part = next_inner(p1, obs, inner)
    p2, to_a, to_b = next_outer(part, a, b, outer)
    a, b = pair_swap(to_a, 0), pair_swap(to_b, 1)
    part = next_inner(p2, obs, inner)
    p3, m = last_outer(part, a, b, outer, p0, p1, p2)
    m = lax.all_to_all(m, "space", 0, 0)
    return finish(m, [p0, p1, p2, p3])


def solution(mesh):
    in_specs = (
        P("member", "space", None),
        P(),
        P("space"),
        P("space", "member"),
        P(None, "space", "member"),
    )
    out_specs = (P(None, "space", "member"), P(None, "space", "member"))
    return jax.shard_map(
        on_device, mesh=mesh, in_specs=in_specs, out_specs=out_specs, check_vma=False
    )
```
